256 devices in a mesh: batch: 16 (over z_hi, x), seq: 16 (over z_lo, y, core).
Axes of the slice: x: 4, y: 4, z: 8 (z_hi: 4, z_lo: 2; z = z_hi * 2 + z_lo), core: 2. Of those that a mesh axis runs over, the one named last changes fastest.
Arguments:
- tower_input: bfloat16 [16, 2048, 1536], P('batch', 'seq'), may hold values from -36 to 36
- norm_gain: float32 [1536], replicated, may hold values from 0.1 to 1.9
- conv_weight: bfloat16 [3, 1536, 768], P(None, 'seq', 'batch'), may hold values from -0.09375 to 0.09375
- mix_weight: bfloat16 [768, 1536], P('batch', 'seq'), may hold values from -0.21875 to 0.21875
- head_weight: bfloat16 [1536, 4096], P(None, 'seq'), may hold values from -0.15625 to 0.15625
- head_bias: float32 [4096], replicated, may hold values from -2 to 1
- pred_cotangent: bfloat16 [16, 2048, 4096], P('batch', 'seq'), may hold values from -6 to 6
Outputs:
- predictions: bfloat16 [16, 2048, 4096], P('batch', 'seq')
- input_grad: bfloat16 [16, 2048, 1536], P('batch', 'seq')
- conv_grad: float32 [3, 1536, 768], P(None, 'seq', 'batch')
- mix_grad: float32 [768, 1536], P('batch', 'seq')
The draws below stay inside these ranges and needn't reach their ends.
All inputs are finite; a program needn't handle non-finite values.
Results may differ from the reference program's by a relative error of at most 0.035.
Values may be sent and summed in bfloat16 or wider, within the bound.
A program may use at most 128 MiB of HBM per device.

```python
import math
import jax
import jax.numpy as jnp
from jax import lax

CH = 1536
INNER = 768
TRACKS = 4096
DILATION_STEP = 8
BINS_DEV = 128
BATCH = 16
SAMPLE_BINS = 2048
TRACKS_DEV = 256
N_SEQ = 16


def draw_tower_input(key, part):
    key_values, key_rows, key_columns = jax.random.split(key, 3)
    values = jnp.clip(jax.random.normal(key_values, (BATCH, SAMPLE_BINS, CH), jnp.float32), -4.0, 4.0)
    lowest_scale = 0.3
    highest_scale = 3.0
    row_scale = jnp.exp(jax.random.uniform(key_rows, (BATCH, SAMPLE_BINS, 1), jnp.float32, math.log(lowest_scale), math.log(highest_scale)))
    column_scale = jnp.exp(jax.random.uniform(key_columns, (1, 1, CH), jnp.float32, math.log(lowest_scale), math.log(highest_scale)))
    return (values * row_scale * column_scale).astype(jnp.bfloat16)


def shard_levels(key, shape, cuts, least, top_value):
    gain = 1.0
    for axis_at, shards_of in cuts:
        heights = jax.random.uniform(jax.random.fold_in(jax.random.fold_in(key, 6), axis_at), (shards_of,), jnp.float32, least / len(cuts), top_value / len(cuts))
        gain = gain * jnp.repeat(jnp.exp(heights), shape[axis_at] // shards_of).reshape((-1,) + (1,) * (len(shape) - 1 - axis_at))
    return gain


def scatter_about(key, shape, spread, limit, cuts=(), dtype=jnp.bfloat16):
    entries = spread * jax.random.normal(key, shape, jnp.float32)
    if cuts:
        entries = entries * shard_levels(key, shape, cuts, -0.22, 0.18)
    return jnp.clip(entries, -limit, limit).astype(dtype)


def setup_inputs(seed: int = 0) -> dict:
    seeds = jax.random.split(jax.random.key(seed), 8)
    return {
        "tower_input": draw_tower_input(jax.random.fold_in(seeds[7], 71), 0),
        "norm_gain": jnp.clip(1.0 + 0.18 * jax.random.normal(seeds[1], (CH,), jnp.float32), 0.1, 1.9),
        "conv_weight": scatter_about(seeds[2], (3, CH, INNER), (3 * CH) ** -0.5, 0.09375, ((1, 16), (2, 16))),
        "mix_weight": scatter_about(seeds[3], (INNER, CH), INNER ** -0.5, 0.21875, ((0, 16), (1, 16))),
        "head_weight": scatter_about(seeds[4], (CH, TRACKS), CH ** -0.5, 0.15625, ((1, 16),)),
        "head_bias": jnp.clip(jax.random.uniform(seeds[5], (TRACKS,), jnp.float32, -2.0, 1.0), -2.0, 1.0),
        "pred_cotangent": scatter_about(seeds[6], (BATCH, SAMPLE_BINS, TRACKS), 1.0, 6.0, ((0, 16), (1, 16))),
    }


def gelu_tanh(values):
    return jax.nn.gelu(values, approximate=True)

def activate(inputs, norm_gain):
    mean_sq = lax.optimization_barrier(jnp.mean(inputs * inputs, axis=-1, keepdims=True))
    return gelu_tanh(inputs * lax.rsqrt(mean_sq + 1e-06) * norm_gain)

def round_sum(terms):
    rounded = lax.optimization_barrier(terms.astype(jnp.bfloat16))
    return lax.optimization_barrier(jnp.sum(rounded.astype(jnp.float32), axis=0))

def reference(tower_input, norm_gain, conv_weight, mix_weight, head_weight, head_bias, pred_cotangent):

    def one_sample(running, sample_pair):
        sample, cotangent = sample_pair
        conv_sum, mix_sum = running
        inputs = sample.astype(jnp.float32)
        gelu_output = activate(inputs, norm_gain).astype(jnp.bfloat16)
        padded_input = jnp.pad(gelu_output, ((DILATION_STEP, DILATION_STEP), (0, 0)))
        kernel_tap_rows = [padded_input[kernel_tap_index * DILATION_STEP:kernel_tap_index * DILATION_STEP + SAMPLE_BINS] for kernel_tap_index in range(3)]
        conv_out = jnp.zeros((SAMPLE_BINS, INNER), jnp.float32)
        for kernel_tap_index in range(3):
            conv_out = conv_out + jnp.dot(kernel_tap_rows[kernel_tap_index], conv_weight[kernel_tap_index], preferred_element_type=jnp.float32)
        hidden = gelu_tanh(conv_out).astype(jnp.bfloat16)
        tower_out = (inputs + jnp.dot(hidden, mix_weight, preferred_element_type=jnp.float32)).astype(jnp.bfloat16)
        logits = jnp.dot(tower_out, head_weight, preferred_element_type=jnp.float32) + head_bias
        predictions = jax.nn.softplus(logits).astype(jnp.bfloat16)
        dlogits = (cotangent.astype(jnp.float32) * jax.nn.sigmoid(logits)).astype(jnp.bfloat16)
        grouped = jnp.einsum('tgk,cgk->gtc', dlogits.reshape(SAMPLE_BINS, N_SEQ, TRACKS_DEV).astype(jnp.float32), head_weight.reshape(CH, N_SEQ, TRACKS_DEV).astype(jnp.float32))
        dtower = round_sum(grouped)
        dtower_half = dtower.astype(jnp.bfloat16)
        dhidden = jnp.dot(dtower_half, mix_weight.T, preferred_element_type=jnp.float32)
        conv_output_gradient = jax.vjp(gelu_tanh, conv_out)[1](dhidden)[0].astype(jnp.bfloat16)
        padded_input_gradient = jnp.pad(conv_output_gradient, ((DILATION_STEP, DILATION_STEP), (0, 0)))
        dactivated = jnp.zeros((SAMPLE_BINS, CH), jnp.float32)
        for kernel_tap_index in range(3):
            shifted_rows = padded_input_gradient[(2 - kernel_tap_index) * DILATION_STEP:(2 - kernel_tap_index) * DILATION_STEP + SAMPLE_BINS]
            dactivated = dactivated + jnp.dot(shifted_rows, conv_weight[kernel_tap_index].T, preferred_element_type=jnp.float32)
        dnorm_path = jax.vjp(lambda values: activate(values, norm_gain), inputs)[1](dactivated)[0]
        input_grad = (dtower + dnorm_path).astype(jnp.bfloat16)
        blocked_grad = conv_output_gradient.reshape(N_SEQ, BINS_DEV, INNER).astype(jnp.float32)
        conv_terms = []
        for kernel_tap_index in range(3):
            blocked_taps = kernel_tap_rows[kernel_tap_index].reshape(N_SEQ, BINS_DEV, CH).astype(jnp.float32)
            conv_terms.append(round_sum(jnp.einsum('jtc,jtd->jcd', blocked_taps, blocked_grad)))
        mix_term = round_sum(jnp.einsum('jtd,jtc->jdc', hidden.reshape(N_SEQ, BINS_DEV, INNER).astype(jnp.float32), dtower_half.reshape(N_SEQ, BINS_DEV, CH).astype(jnp.float32)))
        return ((conv_sum + jnp.stack(conv_terms), mix_sum + mix_term), (predictions, input_grad))
    zero_sums = (jnp.zeros((3, CH, INNER), jnp.float32), jnp.zeros((INNER, CH), jnp.float32))
    sums, outputs = lax.scan(one_sample, zero_sums, (tower_input, pred_cotangent))
    return (outputs[0], outputs[1], sums[0] / BATCH, sums[1] / BATCH)
```

```python
import functools

import jax
import jax.numpy as jnp
from jax import lax
from jax.experimental import pallas as pl
from jax.experimental.pallas import tpu as pltpu
from jax.sharding import PartitionSpec as P

CH = 1536
INNER = 768
TRACKS = 4096
STEP = 8
BINS = 128
BF16 = jnp.bfloat16
F32 = jnp.float32
ROOT = 0.7978845608028654
CUBE = 0.044715
LAST = (((1,), (1,)), ((), ()))
N_COPIES = 260


def place():
    b, s = lax.axis_index("batch"), lax.axis_index("seq")
    return b % 4, (s // 2) % 4, (b // 4) * 2 + s // 8, s % 2


def device(x, y, z, c):
    return ((z // 2) * 4 + x, (z % 2) * 8 + y * 2 + c)


class Copies:
    def __init__(self, send, recv):
        self.send, self.recv, self.sent, self.ids = send, recv, [], {}

    def of(self, src, dst, to, key):
        i = self.ids.setdefault(key, len(self.ids))
        return pltpu.make_async_remote_copy(
            src_ref=src,
            dst_ref=dst,
            send_sem=self.send.at[i],
            recv_sem=self.recv.at[i],
            device_id=to,
            device_id_type=pl.DeviceIdType.MESH,
        )

    def start(self, block, to, key, dst=None):
        copy = self.of(block, block if dst is None else dst, to, key)
        copy.start()
        self.sent.append(copy)

    def arrive(self, block, to, key):
        self.of(block, block, to, key).wait_recv()

    def finish(self):
        for copy in self.sent:
            copy.wait_send()


def meet(x, y, z, c):
    b, s = lax.axis_index("batch"), lax.axis_index("seq")
    others = [device(x, y, z, 1 - c), (b, (s + 1) % 16), (b, (s + 15) % 16)]
    others += [device((x + d) % 4, y, z, c) for d in (1, 2, 3)]
    others += [device(x, (y + d) % 4, z, c) for d in (1, 2, 3)]
    others += [device(x, y, (z + d) % 8, c) for d in range(1, 8)]
    barrier = pltpu.get_barrier_semaphore()
    for other in others:
        pl.semaphore_signal(barrier, inc=1, device_id=other, device_id_type=pl.DeviceIdType.MESH)
    pl.semaphore_wait(barrier, len(others))


def gelu(v):
    return 0.5 * v * (1.0 + jnp.tanh(ROOT * (v + CUBE * v * v * v)))


def gelu_slope(v):
    t = jnp.tanh(ROOT * (v + CUBE * v * v * v))
    return 0.5 * (1.0 + t) + 0.5 * v * (1.0 - t * t) * (ROOT * (1.0 + 3.0 * CUBE * v * v))


def rows_loop(total, step):
    def run(body):
        def one(i, carry):
            body(pl.multiple_of(i * step, step))
            return carry

        lax.fori_loop(0, total // step, one, 0)

    return run


def kernel(
    shard_ref, h_ref, in_ref, gain_ref, bias_ref, cot_ref,
    pred_ref, ig_ref, grad_ref,
    W, H, act, AP, AX, conv, hidden, tower, dtower, DT, DX, dext, dext16, hT, dT, dh2, dact,
    G, RX, RY, RZ, M0, M1, M2, L0, L1, L2, sum0,
    send, recv, local,
):
    x, y, z, c = place()
    b, s = lax.axis_index("batch"), lax.axis_index("seq")
    zl, zh = z % 2, z // 2
    sib = device(x, y, z, 1 - c)
    before, after = (b, (s + 15) % 16), (b, (s + 1) % 16)
    own = [
        pltpu.make_async_copy(shard_ref, W.at[:, zl, y, c, zh, x], local.at[0]),
        pltpu.make_async_copy(h_ref, H.at[zl, y, c], local.at[1]),
    ]
    for copy in own:
        copy.start()
    meet(x, y, z, c)
    copies = Copies(send, recv)
    start, arrive = copies.start, copies.arrive

    def at(dx=0, dy=0, dz=0):
        return device((x + dx) % 4, (y + dy) % 4, (z + dz) % 8, c)

    def shard(dz):
        zz = (z + dz) % 8
        return W.at[:, zz % 2, y, c, zz // 2, x]

    def col(part, dx, dy):
        parts = pl.ds(0, 2) if part == 0 else pl.ds(2, 1)
        return W.at[parts, :, (y + dy) % 4, c, :, (x + dx) % 4]

    def half_col(part, dx, dy, half):
        if part == 0:
            return W.at[half, :, (y + dy) % 4, c, :, (x + dx) % 4]
        return W.at[2, half, (y + dy) % 4, c, :, (x + dx) % 4]

    def head(dzl, dy, half):
        rows = slice(None) if half is None else pl.ds(half * 768, 768)
        return H.at[(zl + dzl) % 2, (y + dy) % 4, c, rows]

    def spread(d):
        start(col(0, 0, d), at(dx=1), ("p3", 0, 1, d % 4))
        start(col(0, 0, d), at(dx=-1), ("p3", 0, 3, d % 4))
        start(col(1, d, 0), at(dy=1), ("p3", 1, 1, d % 4))
        start(col(1, d, 0), at(dy=-1), ("p3", 1, 3, d % 4))
        start(col(0, 0, d), sib, ("s", 0, 0, d % 4))
        start(col(1, d, 0), sib, ("s", 1, 0, d % 4))

    def second_hop(q):
        for d in (1, -1):
            half = 0 if d == 1 else 1
            arrive(col(0, -d, q), sib, ("p3", 0, d % 4, q % 4))
            start(half_col(0, -d, q, half), at(dx=d), ("p4", 0, d % 4, q % 4))
            start(col(0, -d, q), sib, ("s", 0, d % 4, q % 4))
            arrive(col(1, q, -d), sib, ("p3", 1, d % 4, q % 4))
            start(half_col(1, q, -d, half), at(dy=d), ("p4", 1, d % 4, q % 4))
            start(col(1, q, -d), sib, ("s", 1, d % 4, q % 4))

    def last_hop(q):
        for half, d in ((0, 1), (1, -1)):
            arrive(half_col(0, 2, q, half), sib, ("p4", 0, d % 4, q % 4))
            arrive(half_col(1, q, 2, half), sib, ("p4", 1, d % 4, q % 4))
        start(col(0, 2, q), sib, ("s", 0, 2, q % 4))
        start(col(1, q, 2), sib, ("s", 1, 2, q % 4))

    def head_first():
        for d, half in ((1, 0), (-1, 1)):
            arrive(head(0, -d, half), sib, ("hy", d % 4, half))
            start(head(0, -d, half), at(dy=d), ("hy2", d % 4))
            start(head(0, -d, half), at(dz=d), ("hz", d % 8, -d % 4))

    def head_second():
        for d, half in ((1, 0), (-1, 1)):
            arrive(head(0, -d, 1 - half), sib, ("hy", d % 4, 1 - half))
            start(head(0, -d, 1 - half), at(dz=-d), ("hz", -d % 8, -d % 4))
            start(head(0, -d, None), sib, ("hs", 0, -d % 4))

    def head_third():
        arrive(head(0, 2, 0), sib, ("hy2", 1))
        arrive(head(0, 2, 1), sib, ("hy2", 3))
        start(head(0, 2, 0), at(dz=1), ("hz", 1, 2))
        start(head(0, 2, 1), at(dz=-1), ("hz", 7, 2))
        start(head(0, 2, None), sib, ("hs", 0, 2))

    def head_other(dy):
        arrive(head(1, dy, 0), sib, ("hz", 1, dy % 4))
        arrive(head(1, dy, 1), sib, ("hz", 7, dy % 4))
        start(head(1, dy, None), sib, ("hs", 1, dy % 4))

    def from_sib():
        for q in (0, -1, 1, 2):
            for d in (0, 1, -1, 2):
                arrive(W.at[pl.ds(0, 2), :, (y + q) % 4, 1 - c, :, (x - d) % 4], sib, ("s", 0, d % 4, q % 4))
                arrive(W.at[pl.ds(2, 1), :, (y - d) % 4, 1 - c, :, (x + q) % 4], sib, ("s", 1, d % 4, q % 4))

    own[0].wait()
    for dz in (1, -1, 2, -2, 3, -3, 4):
        start(shard(0), at(dz=dz), ("z", dz % 8))
    own[1].wait()
    for half in (0, 1):
        start(head(0, 0, half), at(dy=1), ("hy", 1, half))
        start(head(0, 0, 1 - half), at(dy=-1), ("hy", 3, 1 - half))
    start(head(0, 0, None), sib, ("hs", 0, 0))

    @rows_loop(BINS, 16)
    def _(r):
        v = in_ref[pl.ds(r, 16), :].astype(F32)
        mean_sq = jnp.mean(v * v, axis=-1, keepdims=True)
        a = gelu(v * lax.rsqrt(mean_sq + 1e-06) * gain_ref[...])
        act[pl.ds(r + 8, 16), :] = a.astype(BF16).astype(F32)

    start(act.at[pl.ds(8, 8)], before, ("halo", 0), dst=act.at[pl.ds(136, 8)])
    start(act.at[pl.ds(128, 8)], after, ("halo", 1), dst=act.at[pl.ds(0, 8)])

    for dz in (1, -1, 2, -2, 3, -3, 4):
        arrive(shard(-dz), sib, ("z", dz % 8))
    for d in (1, -1, 2):
        start(col(0, 0, 0), at(dy=d), ("p2", 0, d % 4))
        start(col(1, 0, 0), at(dx=d), ("p2", 1, d % 4))
    spread(0)
    start(head(0, 0, 0), at(dz=1), ("hz", 1, 0))
    start(head(0, 0, 1), at(dz=-1), ("hz", 7, 0))
    for d in (1, -1):
        arrive(col(0, 0, -d), sib, ("p2", 0, d % 4))
        arrive(col(1, -d, 0), sib, ("p2", 1, d % 4))
        spread(-d)
    arrive(act.at[pl.ds(136, 8)], sib, ("halo", 0))
    arrive(act.at[pl.ds(0, 8)], sib, ("halo", 1))

    @pl.when(s == 0)
    def _():
        act[0:8, :] = jnp.zeros((8, CH), F32)

    @pl.when(s == 15)
    def _():
        act[136:144, :] = jnp.zeros((8, CH), F32)

    arrive(col(0, 0, 2), sib, ("p2", 0, 2))
    arrive(col(1, 2, 0), sib, ("p2", 1, 2))
    spread(2)
    head_first()

    @rows_loop(BINS, 16)
    def _(r):
        for q in range(4):
            taps = [act[pl.ds(r + 8 * k, 16), pl.ds(q * 384, 384)] for k in range(3)]
            for i in range(4):
                g = 4 * q + i
                pieces = [t[:, 96 * i : 96 * i + 96] for t in taps] + [jnp.zeros((16, 96), F32)]
                AP[g % 2, g // 2, pl.ds(r, 16), :] = jnp.concatenate(pieces, axis=1).astype(BF16)

    start(AP.at[1 - c], sib, ("ax",), dst=AX)
    second_hop(0)
    second_hop(-1)
    head_second()
    second_hop(1)
    second_hop(2)
    for q in (0, -1, 1, 2):
        last_hop(q)
    head_third()
    from_sib()

    def w(p, j, cc):
        return W[p, j // 4, j % 4, cc].reshape(INNER, 128)

    conv[...] = jnp.zeros_like(conv)

    def conv_step(j, carry):
        lhs = jnp.concatenate([AP[0, j], AP[1, j]], axis=1)
        rhs = jnp.concatenate([w(p, j, cc) for cc in range(2) for p in range(3)], axis=1)
        conv[...] += lax.dot_general(lhs, rhs, LAST, preferred_element_type=F32)
        return carry

    lax.fori_loop(0, 8, conv_step, 0)
    for dy in (0, -1, 1, 2):
        head_other(dy)

    @rows_loop(BINS, 16)
    def _(r):
        hidden[pl.ds(r, 16), :] = gelu(conv[pl.ds(r, 16), :]).astype(BF16)

    start(hidden, sib, ("hidden",), dst=dh2.at[0])

    for q in range(4):
        mixed = []
        for i in range(2):
            j = 2 * q + i
            rhs = jnp.concatenate([w(2, j, 0), w(2, j, 1)], axis=1)
            m = jnp.dot(hidden[...], rhs, preferred_element_type=F32)
            mixed += [m[:, 32:128], m[:, 160:256]]
        lanes = slice(384 * q, 384 * q + 384)
        tower[:, lanes] = (in_ref[:, lanes].astype(F32) + jnp.concatenate(mixed, axis=1)).astype(BF16)

    dtower[...] = jnp.zeros_like(dtower)

    def head_step(zz, yy, cc):
        lanes = pl.ds(pl.multiple_of((zz * 8 + yy * 2 + cc) * 256, 256), 256)
        weight = H[zz, yy, cc]
        logits = jnp.dot(tower[...], weight, preferred_element_type=F32) + bias_ref[:, lanes]
        e = jnp.exp(-jnp.abs(logits))
        pred_ref[:, lanes] = (jnp.maximum(logits, 0.0) + jnp.log1p(e)).astype(BF16)
        sigmoid = jnp.where(logits >= 0.0, 1.0, e) / (1.0 + e)
        dlogits = (cot_ref[:, lanes].astype(F32) * sigmoid).astype(BF16)
        dtower[...] += lax.dot_general(dlogits, weight, LAST, preferred_element_type=F32)

    for cc in (0, 1):
        for dzl in (0, 1):
            for dy in (0, -1, 1, 2):
                piece = H.at[(zl + dzl) % 2, (y + dy) % 4, (c + cc) % 2]
                if cc == 1:
                    arrive(piece, sib, ("hs", dzl, dy % 4))

    def head_loop(g, carry):
        head_step(g // 8, (g // 2) % 4, g % 2)
        return carry

    lax.fori_loop(0, 16, head_loop, 0)

    @rows_loop(BINS, 16)
    def _(r):
        for q in range(4):
            v = dtower[pl.ds(r, 16), pl.ds(q * 384, 384)]
            for i in range(4):
                g = 4 * q + i
                pieces = [jnp.zeros((16, 32), F32), v[:, 96 * i : 96 * i + 96]]
                DT[g % 2, g // 2, pl.ds(r, 16), :] = jnp.concatenate(pieces, axis=1).astype(BF16)

    start(DT.at[1 - c], sib, ("dt",), dst=DX)
    sum0[...] = jnp.zeros_like(sum0)

    def dhidden_step(j, carry):
        lhs = jnp.concatenate([DT[0, j], DT[1, j]], axis=1)
        rhs = jnp.concatenate([w(2, j, 0), w(2, j, 1)], axis=1)
        sum0[...] += lax.dot_general(lhs, rhs, LAST, preferred_element_type=F32)
        return carry

    lax.fori_loop(0, 8, dhidden_step, 0)

    @rows_loop(BINS, 16)
    def _(r):
        d = sum0[pl.ds(r, 16), :] * gelu_slope(conv[pl.ds(r, 16), :])
        half = d.astype(BF16)
        dh2[2, pl.ds(r, 16), :] = half
        dext[pl.ds(r + 8, 16), :] = half.astype(F32)

    start(dh2.at[2], sib, ("dconv",), dst=dh2.at[1])
    start(dext.at[pl.ds(8, 8)], before, ("dhalo", 0), dst=dext.at[pl.ds(136, 8)])
    start(dext.at[pl.ds(128, 8)], after, ("dhalo", 1), dst=dext.at[pl.ds(0, 8)])

    arrive(dh2.at[0], sib, ("hidden",))
    arrive(dh2.at[1], sib, ("dconv",))
    arrive(AX, sib, ("ax",))
    arrive(DX, sib, ("dt",))
    hT[:, 0:128] = hidden[...].T
    hT[:, 128:256] = dh2[0].T
    dT[:, 0:128] = dh2[2].T
    dT[:, 128:256] = dh2[1].T

    def grad_step(j, carry):
        rhs = jnp.concatenate([AP[c, j], AX[j]], axis=0)
        g = jnp.dot(dT[...], rhs, preferred_element_type=F32)
        more = jnp.dot(hT[...], jnp.concatenate([DT[c, j], DX[j]], axis=0), preferred_element_type=F32)
        for p in range(3):
            part = g[:, 128 * p : 128 * p + 128]
            if p == 2:
                part = part + more
            G[p, j // 4, j % 4] = part.astype(BF16).reshape(4, 4, 48, 128)
        return carry

    lax.fori_loop(0, 8, grad_step, 0)

    def dact_prepare():
        arrive(dext.at[pl.ds(136, 8)], sib, ("dhalo", 0))
        arrive(dext.at[pl.ds(0, 8)], sib, ("dhalo", 1))

        @pl.when(s == 0)
        def _():
            dext[0:8, :] = jnp.zeros((8, INNER), F32)

        @pl.when(s == 15)
        def _():
            dext[136:144, :] = jnp.zeros((8, INNER), F32)

        dext16[...] = dext[...].astype(BF16)

    def dact_part(q):
        pieces = []
        for i in range(2):
            j = 2 * q + i
            for cc in range(2):
                rhs = jnp.concatenate([w(p, j, cc) for p in range(3)], axis=1)
                d = jnp.dot(dext16[...], rhs, preferred_element_type=F32)
                pieces.append(d[16:144, 0:96] + d[8:136, 96:192] + d[0:128, 192:288])
        dact[:, 384 * q : 384 * q + 384] = jnp.concatenate(pieces, axis=1)

    def dact_finish():
        @rows_loop(BINS, 16)
        def _(r):
            v = in_ref[pl.ds(r, 16), :].astype(F32)
            rs = lax.rsqrt(jnp.mean(v * v, axis=-1, keepdims=True) + 1e-06)
            gain = gain_ref[...]
            dz = dact[pl.ds(r, 16), :] * gelu_slope(v * rs * gain) * gain
            dot = jnp.mean(dz * v, axis=-1, keepdims=True)
            ig = dtower[pl.ds(r, 16), :] + dz * rs - v * (rs * rs * rs * dot)
            ig_ref[pl.ds(r, 16), :] = ig.astype(BF16)

    jobs = [dact_prepare] + [functools.partial(dact_part, q) for q in range(4)] + [dact_finish]

    def half_x(m, h):
        return G.at[0, h, :, :, (x + m) % 4]

    def half_y(m, h):
        return G.at[1, h, (y + m) % 4]

    def half_z(m, h):
        zz = (z + m) % 8
        return G.at[2, zz % 2, pl.ds(2 * h, 2), zz // 2]

    def slots(ring):
        return [(0, m) for m in range(ring, 0, -1)], [(1, m) for m in range(ring - 1, 0, -1)]

    def order(n):
        seq = []
        for m in range(n // 2, 0, -1):
            seq.append((0, m))
            if m > 1:
                seq.append((1, m - 1))
        return seq

    rings = {"x": (4, half_x, RX, "dx"), "y": (4, half_y, RY, "dy"), "z": (8, half_z, RZ, "dz")}

    def ring_send(ax, d, k):
        n, block, buf, name = rings[ax]
        h, m = order(n)[k]
        h = h if d < 0 else 1 - h
        start(block(d * m, h), at(**{name: d}), ("r" + ax, d, k), dst=buf.at[(d + 1) // 2, k])

    def add(dst, srcs):
        total = dst[...].astype(F32)
        for src in srcs:
            total = total + src[...].astype(F32)
        dst[...] = total.astype(BF16)

    def ring_receive(ax, d, k):
        n, block, buf, name = rings[ax]
        seq = order(n)
        h, m = seq[k]
        slot = buf.at[(d + 1) // 2, k]
        arrive(slot, sib, ("r" + ax, d, k))
        mine = h if d < 0 else 1 - h
        add(block(d * (m - 1), mine), [slot])
        if m > 1:
            ring_send(ax, d, seq.index((h, m - 1)))

    for ax in "xyz":
        for d in (-1, 1):
            ring_send(ax, d, 0)
            ring_send(ax, d, 1)
    jobs.pop(0)()
    jobs.pop(0)()

    def both(ax, k):
        for d in (-1, 1):
            ring_receive(ax, d, k)

    both("z", 0)
    both("x", 0)
    both("y", 0)
    both("z", 1)
    jobs.pop(0)()
    both("z", 2)
    both("x", 1)
    both("y", 1)
    both("z", 3)
    jobs.pop(0)()
    both("z", 4)
    both("x", 2)
    both("y", 2)

    def mid_send(p, d):
        if p == 0:
            start(G.at[0, :, (y + d) % 4, :, x], at(dy=d), ("m", 0, d), dst=M0.at[d - 1])
        elif p == 1:
            start(G.at[1, :, y, :, (x + d) % 4], at(dx=d), ("m", 1, d), dst=M1.at[d - 1])
        else:
            start(G.at[2, zl, :, zh, (x + d) % 4], at(dx=d), ("m", 2, d), dst=M2.at[d - 1])

    def mid_receive(p):
        buf = (M0, M1, M2)[p]
        for d in (1, 2, 3):
            arrive(buf.at[d - 1], sib, ("m", p, d))
        home = (G.at[0, :, y, :, x], G.at[1, :, y, :, x], G.at[2, zl, :, zh, x])[p]
        add(home, [buf.at[d] for d in range(3)])

    for p in (0, 1):
        for d in (1, 2, 3):
            mid_send(p, d)
    both("z", 5)
    both("z", 6)
    for d in (1, 2, 3):
        mid_send(2, d)
    jobs.pop(0)()

    def last_send(p, d):
        if p < 2:
            zz = (z + d) % 8
            start(G.at[p, zz % 2, y, zz // 2, x], at(dz=d), ("l", p, d), dst=(L0, L1)[p].at[d - 1])
        else:
            start(G.at[2, zl, (y + d) % 4, zh, x], at(dy=d), ("l", 2, d), dst=L2.at[d - 1])

    def last_receive(p):
        buf, n = ((L0, 7), (L1, 7), (L2, 3))[p]
        for d in range(n):
            arrive(buf.at[d], sib, ("l", p, d + 1))
        total = G[p, zl, y, zh, x].astype(F32)
        for d in range(n):
            total = total + buf[d].astype(F32)
        grad_ref[p] = total * (1.0 / 16.0)

    for p in (0, 1):
        mid_receive(p)
        for d in range(1, 8):
            last_send(p, d)
    mid_receive(2)
    for d in (1, 2, 3):
        last_send(2, d)
    while jobs:
        jobs.pop(0)()
    for p in range(3):
        last_receive(p)
    copies.finish()
    assert len(copies.ids) <= N_COPIES, len(copies.ids)


def body(tower_input, norm_gain, conv_weight, mix_weight, head_weight, head_bias, pred_cotangent):
    shard = jnp.concatenate([conv_weight.transpose(2, 0, 1), mix_weight[:, None, :]], axis=1)
    shard = shard.reshape(48, 3, 128).transpose(1, 0, 2)
    vmem = pl.BlockSpec(memory_space=pltpu.VMEM)
    hbm = pl.BlockSpec(memory_space=pl.ANY)
    scratch = [
        ((3, 2, 4, 2, 4, 4, 48, 128), BF16),
        ((2, 4, 2, CH, 256), BF16),
        ((BINS + 16, CH), F32),
        ((2, 8, BINS, 384), BF16),
        ((8, BINS, 384), BF16),
        ((BINS, INNER), F32),
        ((BINS, INNER), BF16),
        ((BINS, CH), BF16),
        ((BINS, CH), F32),
        ((2, 8, BINS, 128), BF16),
        ((8, BINS, 128), BF16),
        ((BINS + 16, INNER), F32),
        ((BINS + 16, INNER), BF16),
        ((INNER, 256), BF16),
        ((INNER, 256), BF16),
        ((3, BINS, INNER), BF16),
        ((BINS, CH), F32),
        ((3, 2, 4, 4, 4, 48, 128), BF16),
        ((2, 3, 4, 4, 48, 128), BF16),
        ((2, 3, 4, 4, 48, 128), BF16),
        ((2, 7, 2, 4, 48, 128), BF16),
        ((3, 2, 4, 48, 128), BF16),
        ((3, 2, 4, 48, 128), BF16),
        ((3, 4, 48, 128), BF16),
        ((7, 48, 128), BF16),
        ((7, 48, 128), BF16),
        ((3, 48, 128), BF16),
        ((BINS, INNER), F32),
    ]
    predictions, input_grad, grads = pl.pallas_call(
        kernel,
        out_shape=[
            jax.ShapeDtypeStruct((BINS, TRACKS), BF16),
            jax.ShapeDtypeStruct((BINS, CH), BF16),
            jax.ShapeDtypeStruct((3, 48, 128), F32),
        ],
        in_specs=[hbm, hbm, vmem, vmem, vmem, vmem],
        out_specs=[vmem, vmem, vmem],
        scratch_shapes=[pltpu.VMEM(*spec) for spec in scratch]
        + [
            pltpu.SemaphoreType.DMA((N_COPIES,)),
            pltpu.SemaphoreType.DMA((N_COPIES,)),
            pltpu.SemaphoreType.DMA((2,)),
        ],
        compiler_params=pltpu.CompilerParams(
            collective_id=0, has_side_effects=True, vmem_limit_bytes=60 * 2**20
        ),
        name="block",
    )(
        shard,
        head_weight,
        tower_input[0],
        norm_gain.reshape(1, CH),
        head_bias.reshape(1, TRACKS),
        pred_cotangent[0],
    )
    grads = grads.transpose(1, 0, 2).reshape(48, 4, 96)
    conv_grad = grads[:, :3].transpose(1, 2, 0)
    mix_grad = grads[:, 3]
    return (predictions[None], input_grad[None], conv_grad, mix_grad)


def solution(mesh):
    in_specs = (
        P("batch", "seq", None),
        P(),
        P(None, "seq", "batch"),
        P("batch", "seq"),
        P(None, "seq"),
        P(),
        P("batch", "seq", None),
    )
    out_specs = (
        P("batch", "seq", None),
        P("batch", "seq", None),
        P(None, "seq", "batch"),
        P("batch", "seq"),
    )
    return jax.shard_map(body, mesh=mesh, in_specs=in_specs, out_specs=out_specs, check_vma=False)
```

```python
import functools

import jax
import jax.numpy as jnp
from jax import lax
from jax.experimental import pallas as pl
from jax.experimental.pallas import tpu as pltpu
from jax.sharding import PartitionSpec as P

CH = 1536
INNER = 768
TRACKS = 4096
STEP = 8
BINS = 128
BF16 = jnp.bfloat16
F32 = jnp.float32
ROOT = 0.7978845608028654
CUBE = 0.044715
LAST = (((1,), (1,)), ((), ()))
N_COPIES = 137


def place():
    b, s = lax.axis_index("batch"), lax.axis_index("seq")
    return b % 4, (s // 2) % 4, (b // 4) * 2 + s // 8, s % 2


def device(x, y, z, c):
    return ((z // 2) * 4 + x, (z % 2) * 8 + y * 2 + c)


class Copies:
    def __init__(self, send, recv):
        self.send, self.recv, self.sent, self.ids = send, recv, [], {}

    def of(self, src, dst, to, key):
        i = self.ids.setdefault(key, len(self.ids))
        return pltpu.make_async_remote_copy(
            src_ref=src,
            dst_ref=dst,
            send_sem=self.send.at[i],
            recv_sem=self.recv.at[i],
            device_id=to,
            device_id_type=pl.DeviceIdType.MESH,
        )

    def start(self, block, to, key, dst=None):
        copy = self.of(block, block if dst is None else dst, to, key)
        copy.start()
        self.sent.append(copy)

    def arrive(self, block, to, key):
        self.of(block, block, to, key).wait_recv()

    def group(self, block, to, key):
        self.of(block, block, to, key).start()

    def finish(self):
        for copy in self.sent:
            copy.wait_send()


def meet(x, y, z, c):
    b, s = lax.axis_index("batch"), lax.axis_index("seq")
    others = [device(x, y, z, 1 - c), (b, (s + 1) % 16), (b, (s + 15) % 16)]
    others += [device((x + d) % 4, y, z, c) for d in (1, 2, 3)]
    others += [device(x, (y + d) % 4, z, c) for d in (1, 2, 3)]
    others += [device(x, y, (z + d) % 8, c) for d in range(1, 8)]
    barrier = pltpu.get_barrier_semaphore()
    for other in others:
        pl.semaphore_signal(barrier, inc=1, device_id=other, device_id_type=pl.DeviceIdType.MESH)
    pl.semaphore_wait(barrier, len(others))


def gelu(v):
    return 0.5 * v * (1.0 + jnp.tanh(ROOT * (v + CUBE * v * v * v)))


def gelu_slope(v):
    t = jnp.tanh(ROOT * (v + CUBE * v * v * v))
    return 0.5 * (1.0 + t) + 0.5 * v * (1.0 - t * t) * (ROOT * (1.0 + 3.0 * CUBE * v * v))


def rows_loop(total, step):
    def run(body):
        def one(i, carry):
            body(pl.multiple_of(i * step, step))
            return carry

        lax.fori_loop(0, total // step, one, 0)

    return run


def kernel(
    taps_ref, mix_ref, h_ref, in_ref, gain_ref, bias_ref, cot_ref,
    pred_out, ig_ref, grad_ref,
    W, H, act, AP, AX, conv, hidden, tower, dtower, DT, DX, dext, dext16, hT, dT, dh2, dact,
    pred_ref, G, RX, RY, RZ, M0, M1, M2, L0, L1, L2, sum0,
    send, recv, local,
):
    x, y, z, c = place()
    b, s = lax.axis_index("batch"), lax.axis_index("seq")
    zl, zh = z % 2, z // 2
    sib = device(x, y, z, 1 - c)
    before, after = (b, (s + 15) % 16), (b, (s + 1) % 16)
    own = pltpu.make_async_copy(h_ref, H.at[zl, y, c], local.at[0])
    own.start()
    packed = [taps_ref[k].astype(F32) for k in range(3)] + [mix_ref[...].astype(F32)]
    packed = jnp.concatenate(packed, axis=1).astype(BF16)
    for p in range(3):
        t = 3 * zl + p if p < 2 else 5 - 3 * zl
        W[t, y, c, zh, x] = packed[:, 128 * p : 128 * p + 128]
    meet(x, y, z, c)
    copies = Copies(send, recv)
    start, arrive = copies.start, copies.arrive

    def at(dx=0, dy=0, dz=0):
        return device((x + dx) % 4, (y + dy) % 4, (z + dz) % 8, c)

    def shard(part, dz):
        zz = (z + dz) % 8
        t = pl.ds(3 * (zz % 2), 2) if part == 0 else pl.ds(5 - 3 * (zz % 2), 1)
        return W.at[t, y, c, zz // 2, x]

    def col(part, dx, dy, core=c):
        t = pl.ds(0, 5) if part == 0 else pl.ds(5, 1)
        return W.at[t, (y + dy) % 4, core, :, (x + dx) % 4]

    def half_col(part, dx, dy, half):
        if part == 0:
            cut = 3 if dy in (0, 1) else 2
            t = pl.ds(0, cut) if half == 0 else pl.ds(cut, 5 - cut)
            return W.at[t, (y + dy) % 4, c, :, (x + dx) % 4]
        return W.at[5, (y + dy) % 4, c, pl.ds(2 * half, 2), (x + dx) % 4]

    def mid_half(part, at_d, d):
        zhs = pl.ds(0, 2) if d == 1 else pl.ds(2, 2)
        if part == 0:
            return W.at[pl.ds(0, 5), (y + at_d) % 4, c, zhs, x]
        return W.at[5, y, c, zhs, (x + at_d) % 4]

    def head(dzl, dy, half):
        rows = slice(None) if half is None else pl.ds(half * 768, 768)
        return H.at[(zl + dzl) % 2, (y + dy) % 4, c, rows]

    def spread(d):
        start(col(0, 0, d), at(dx=1), ("p3", 0, 1, d % 4))
        start(col(0, 0, d), at(dx=-1), ("p3", 0, 3, d % 4))
        start(col(1, d, 0), at(dy=1), ("p3", 1, 1, d % 4))
        start(col(1, d, 0), at(dy=-1), ("p3", 1, 3, d % 4))
        copies.group(col(0, 0, d), sib, ("s",))
        copies.group(col(1, d, 0), sib, ("s",))

    def second_hop(q):
        for d in (1, -1):
            half = 0 if d == 1 else 1
            arrive(col(0, -d, q), sib, ("p3", 0, d % 4, q % 4))
            start(half_col(0, -d, q, half), at(dx=d), ("p4", 0, d % 4, q % 4))
            copies.group(col(0, -d, q), sib, ("s",))
            arrive(col(1, q, -d), sib, ("p3", 1, d % 4, q % 4))
            start(half_col(1, q, -d, half), at(dy=d), ("p4", 1, d % 4, q % 4))
            copies.group(col(1, q, -d), sib, ("s",))

    def last_hop(q):
        for half, d in ((0, 1), (1, -1)):
            arrive(half_col(0, 2, q, half), sib, ("p4", 0, d % 4, q % 4))
            arrive(half_col(1, q, 2, half), sib, ("p4", 1, d % 4, q % 4))
        copies.group(col(0, 2, q), sib, ("s",))
        copies.group(col(1, q, 2), sib, ("s",))

    def head_own(first):
        for d, half in ((1, 0), (-1, 1)):
            half = half if first else 1 - half
            start(head(0, 0, half), at(dy=d), ("hy", d % 4, half))

    def head_first():
        for d, half in ((1, 0), (-1, 1)):
            arrive(head(0, -d, half), sib, ("hy", d % 4, half))
            start(head(0, -d, half), at(dz=d), ("hz", d % 8, -d % 4))

    def head_on():
        for d, half in ((1, 0), (-1, 1)):
            start(head(0, -d, half), at(dy=d), ("hy2", d % 4))

    def head_second():
        for d, half in ((1, 0), (-1, 1)):
            arrive(head(0, -d, 1 - half), sib, ("hy", d % 4, 1 - half))
            start(head(0, -d, 1 - half), at(dz=-d), ("hz", -d % 8, -d % 4))
            start(head(0, -d, None), sib, ("hs", 0, -d % 4))

    def head_third():
        arrive(head(0, 2, 0), sib, ("hy2", 1))
        start(head(0, 2, 0), at(dz=1), ("hz", 1, 2))
        arrive(head(0, 2, 1), sib, ("hy2", 3))
        start(head(0, 2, 1), at(dz=-1), ("hz", 7, 2))
        start(head(0, 2, None), sib, ("hs", 0, 2))

    def head_other(dy):
        arrive(head(1, dy, 0), sib, ("hz", 1, dy % 4))
        arrive(head(1, dy, 1), sib, ("hz", 7, dy % 4))
        start(head(1, dy, None), sib, ("hs", 1, dy % 4))

    def from_sib():
        arrive(W.at[:, :, 1 - c], sib, ("s",))

    for dz in (1, -1, 2, -2, 3, -3, 4):
        start(shard(0, 0), at(dz=dz), ("z", 0, dz % 8))
        start(shard(1, 0), at(dz=dz), ("z", 1, dz % 8))
    own.wait()
    head_own(True)
    start(head(0, 0, None), sib, ("hs", 0, 0))

    @rows_loop(BINS, 16)
    def _(r):
        v = in_ref[pl.ds(r, 16), :].astype(F32)
        mean_sq = jnp.mean(v * v, axis=-1, keepdims=True)
        a = gelu(v * lax.rsqrt(mean_sq + 1e-06) * gain_ref[...].reshape(1, CH))
        act[pl.ds(r + 8, 16), :] = a.astype(BF16).astype(F32)

    start(act.at[pl.ds(8, 8)], before, ("halo", 0), dst=act.at[pl.ds(136, 8)])
    start(act.at[pl.ds(128, 8)], after, ("halo", 1), dst=act.at[pl.ds(0, 8)])

    for dz in (1, -1, 2, -2, 3, -3, 4):
        arrive(shard(0, -dz), sib, ("z", 0, dz % 8))
        arrive(shard(1, -dz), sib, ("z", 1, dz % 8))
    for d in (1, -1):
        start(col(0, 0, 0), at(dy=d), ("p2", 0, d % 4))
        start(col(1, 0, 0), at(dx=d), ("p2", 1, d % 4))
    spread(0)
    start(head(0, 0, 0), at(dz=1), ("hz", 1, 0))
    start(head(0, 0, 1), at(dz=-1), ("hz", 7, 0))
    head_first()
    for d in (1, -1):
        arrive(col(0, 0, -d), sib, ("p2", 0, d % 4))
        start(mid_half(0, -d, d), at(dy=d), ("p2r", 0, d % 4))
        arrive(col(1, -d, 0), sib, ("p2", 1, d % 4))
        start(mid_half(1, -d, d), at(dx=d), ("p2r", 1, d % 4))
        spread(-d)
    second_hop(0)
    head_own(False)
    arrive(act.at[pl.ds(136, 8)], sib, ("halo", 0))
    arrive(act.at[pl.ds(0, 8)], sib, ("halo", 1))

    @pl.when(s == 0)
    def _():
        act[0:8, :] = jnp.zeros((8, CH), F32)

    @pl.when(s == 15)
    def _():
        act[136:144, :] = jnp.zeros((8, CH), F32)

    for d in (1, -1):
        arrive(mid_half(0, 2, d), sib, ("p2r", 0, d % 4))
        arrive(mid_half(1, 2, d), sib, ("p2r", 1, d % 4))
    spread(2)
    head_on()

    @rows_loop(BINS, 16)
    def _(r):
        for q in range(4):
            taps = [act[pl.ds(r + 8 * k, 16), pl.ds(q * 384, 384)] for k in range(3)]
            for i in range(4):
                g = 4 * q + i
                pieces = [t[:, 96 * i : 96 * i + 96] for t in taps] + [jnp.zeros((16, 96), F32)]
                AP[g % 2, g // 2, pl.ds(r, 16), :] = jnp.concatenate(pieces, axis=1).astype(BF16)

    start(AP.at[1 - c], sib, ("ax",), dst=AX)
    last_hop(0)
    head_second()
    second_hop(-1)
    second_hop(1)
    second_hop(2)
    head_third()
    last_hop(-1)
    last_hop(1)
    last_hop(2)
    from_sib()

    def w(p, j, cc):
        t = 3 * (j // 4) + p if p < 2 else 5 - 3 * (j // 4)
        return W[t, j % 4, cc].reshape(INNER, 128)

    conv[...] = jnp.zeros_like(conv)

    def conv_step(j, carry):
        lhs = jnp.concatenate([AP[0, j], AP[1, j]], axis=1)
        rhs = jnp.concatenate([w(p, j, cc) for cc in range(2) for p in range(3)], axis=1)
        conv[...] += lax.dot_general(lhs, rhs, LAST, preferred_element_type=F32)
        return carry

    lax.fori_loop(0, 8, conv_step, 0)
    for dy in (0, -1, 1, 2):
        head_other(dy)

    @rows_loop(BINS, 16)
    def _(r):
        hidden[pl.ds(r, 16), :] = gelu(conv[pl.ds(r, 16), :]).astype(BF16)

    start(hidden, sib, ("hidden",), dst=dh2.at[0])

    for q in range(4):
        mixed = []
        for i in range(2):
            j = 2 * q + i
            rhs = jnp.concatenate([w(2, j, 0), w(2, j, 1)], axis=1)
            m = jnp.dot(hidden[...], rhs, preferred_element_type=F32)
            mixed += [m[:, 32:128], m[:, 160:256]]
        lanes = slice(384 * q, 384 * q + 384)
        tower[:, lanes] = (in_ref[:, lanes].astype(F32) + jnp.concatenate(mixed, axis=1)).astype(BF16)

    dtower[...] = jnp.zeros_like(dtower)

    def head_step(zz, yy):
        lanes = pl.ds(pl.multiple_of((zz * 4 + yy) * 512, 512), 512)
        weight = jnp.concatenate([H[zz, yy, 0], H[zz, yy, 1]], axis=1)
        logits = jnp.dot(tower[...], weight, preferred_element_type=F32) + bias_ref[lanes].reshape(1, -1)
        e = jnp.exp(-jnp.abs(logits))
        pred_ref[:, lanes] = (jnp.maximum(logits, 0.0) + jnp.log1p(e)).astype(BF16)
        sigmoid = jnp.where(logits >= 0.0, 1.0, e) / (1.0 + e)
        dlogits = (cot_ref[:, lanes].astype(F32) * sigmoid).astype(BF16)
        dtower[...] += lax.dot_general(dlogits, weight, LAST, preferred_element_type=F32)

    def ready(dzl, dy):
        arrive(H.at[(zl + dzl) % 2, (y + dy) % 4, 1 - c], sib, ("hs", dzl, dy % 4))

    for dy in (0, -1, 1, 2):
        ready(0, dy)

    def head_loop(dzl):
        def one(j, carry):
            head_step((zl + dzl) % 2, j)
            return carry

        lax.fori_loop(0, 4, one, 0)

    head_loop(0)
    for dy in (0, -1, 1, 2):
        ready(1, dy)
    head_loop(1)
    out = pltpu.make_async_copy(pred_ref, pred_out, local.at[1])
    out.start()

    @rows_loop(BINS, 16)
    def _(r):
        for q in range(4):
            v = dtower[pl.ds(r, 16), pl.ds(q * 384, 384)]
            for i in range(4):
                g = 4 * q + i
                pieces = [jnp.zeros((16, 32), F32), v[:, 96 * i : 96 * i + 96]]
                DT[g % 2, g // 2, pl.ds(r, 16), :] = jnp.concatenate(pieces, axis=1).astype(BF16)

    start(DT.at[1 - c], sib, ("dt",), dst=DX)
    sum0[...] = jnp.zeros_like(sum0)

    def dhidden_step(j, carry):
        lhs = jnp.concatenate([DT[0, j], DT[1, j]], axis=1)
        rhs = jnp.concatenate([w(2, j, 0), w(2, j, 1)], axis=1)
        sum0[...] += lax.dot_general(lhs, rhs, LAST, preferred_element_type=F32)
        return carry

    lax.fori_loop(0, 8, dhidden_step, 0)

    @rows_loop(BINS, 16)
    def _(r):
        d = sum0[pl.ds(r, 16), :] * gelu_slope(conv[pl.ds(r, 16), :])
        half = d.astype(BF16)
        dh2[2, pl.ds(r, 16), :] = half
        dext[pl.ds(r + 8, 16), :] = half.astype(F32)

    start(dh2.at[2], sib, ("dconv",), dst=dh2.at[1])
    start(dext.at[pl.ds(8, 8)], before, ("dhalo", 0), dst=dext.at[pl.ds(136, 8)])
    start(dext.at[pl.ds(128, 8)], after, ("dhalo", 1), dst=dext.at[pl.ds(0, 8)])

    arrive(dh2.at[0], sib, ("hidden",))
    arrive(dh2.at[1], sib, ("dconv",))
    arrive(AX, sib, ("ax",))
    arrive(DX, sib, ("dt",))
    hT[:, 0:128] = hidden[...].T
    hT[:, 128:256] = dh2[0].T
    dT[:, 0:128] = dh2[2].T
    dT[:, 128:256] = dh2[1].T

    def grad_step(j, carry):
        rhs = jnp.concatenate([AP[c, j], AX[j]], axis=0)
        g = jnp.dot(dT[...], rhs, preferred_element_type=F32)
        more = jnp.dot(hT[...], jnp.concatenate([DT[c, j], DX[j]], axis=0), preferred_element_type=F32)
        for p in range(3):
            part = g[:, 128 * p : 128 * p + 128]
            if p == 2:
                part = part + more
            G[p, j // 4, j % 4] = part.astype(BF16).reshape(4, 4, 48, 128)
        return carry

    lax.fori_loop(0, 8, grad_step, 0)

    def dact_prepare():
        arrive(dext.at[pl.ds(136, 8)], sib, ("dhalo", 0))
        arrive(dext.at[pl.ds(0, 8)], sib, ("dhalo", 1))

        @pl.when(s == 0)
        def _():
            dext[0:8, :] = jnp.zeros((8, INNER), F32)

        @pl.when(s == 15)
        def _():
            dext[136:144, :] = jnp.zeros((8, INNER), F32)

        dext16[...] = dext[...].astype(BF16)

    def dact_part(q):
        pieces = []
        for i in range(2):
            j = 2 * q + i
            for cc in range(2):
                rhs = jnp.concatenate([w(p, j, cc) for p in range(3)], axis=1)
                d = jnp.dot(dext16[...], rhs, preferred_element_type=F32)
                pieces.append(d[16:144, 0:96] + d[8:136, 96:192] + d[0:128, 192:288])
        dact[:, 384 * q : 384 * q + 384] = jnp.concatenate(pieces, axis=1)

    def dact_finish():
        @rows_loop(BINS, 16)
        def _(r):
            v = in_ref[pl.ds(r, 16), :].astype(F32)
            rs = lax.rsqrt(jnp.mean(v * v, axis=-1, keepdims=True) + 1e-06)
            gain = gain_ref[...].reshape(1, CH)
            dz = dact[pl.ds(r, 16), :] * gelu_slope(v * rs * gain) * gain
            dot = jnp.mean(dz * v, axis=-1, keepdims=True)
            ig = dtower[pl.ds(r, 16), :] + dz * rs - v * (rs * rs * rs * dot)
            ig_ref[pl.ds(r, 16), :] = ig.astype(BF16)

    jobs = [dact_prepare] + [functools.partial(dact_part, q) for q in range(4)] + [dact_finish]

    def half_x(m, h):
        return G.at[0, h, :, :, (x + m) % 4]

    def half_y(m, h):
        return G.at[1, h, (y + m) % 4]

    def half_z(m, h):
        zz = (z + m) % 8
        return G.at[2, zz % 2, pl.ds(2 * h, 2), zz // 2]

    def slots(ring):
        return [(0, m) for m in range(ring, 0, -1)], [(1, m) for m in range(ring - 1, 0, -1)]

    def order(n):
        seq = []
        for m in range(n // 2, 0, -1):
            seq.append((0, m))
            if m > 1:
                seq.append((1, m - 1))
        return seq

    rings = {"x": (4, half_x, RX, "dx"), "y": (4, half_y, RY, "dy"), "z": (8, half_z, RZ, "dz")}

    def ring_send(ax, d, k):
        n, block, buf, name = rings[ax]
        h, m = order(n)[k]
        h = h if d < 0 else 1 - h
        start(block(d * m, h), at(**{name: d}), ("r" + ax, d, k), dst=buf.at[(d + 1) // 2, k])

    def add(dst, srcs):
        total = dst[...].astype(F32)
        for src in srcs:
            total = total + src[...].astype(F32)
        dst[...] = total.astype(BF16)

    def ring_receive(ax, d, k):
        n, block, buf, name = rings[ax]
        seq = order(n)
        h, m = seq[k]
        slot = buf.at[(d + 1) // 2, k]
        arrive(slot, sib, ("r" + ax, d, k))
        mine = h if d < 0 else 1 - h
        add(block(d * (m - 1), mine), [slot])
        if m > 1:
            ring_send(ax, d, seq.index((h, m - 1)))

    for ax in "xyz":
        for d in (-1, 1):
            ring_send(ax, d, 0)
            ring_send(ax, d, 1)
    jobs.pop(0)()
    jobs.pop(0)()

    def both(ax, k):
        for d in (-1, 1):
            ring_receive(ax, d, k)

    both("z", 0)
    both("x", 0)
    both("y", 0)
    both("z", 1)
    jobs.pop(0)()
    both("z", 2)
    both("x", 1)
    both("y", 1)
    both("z", 3)
    jobs.pop(0)()
    both("z", 4)
    both("x", 2)
    both("y", 2)

    def mid_send(p, d):
        if p == 0:
            start(G.at[0, :, (y + d) % 4, :, x], at(dy=d), ("m", 0, d), dst=M0.at[d - 1])
        elif p == 1:
            start(G.at[1, :, y, :, (x + d) % 4], at(dx=d), ("m", 1, d), dst=M1.at[d - 1])
        else:
            start(G.at[2, zl, :, zh, (x + d) % 4], at(dx=d), ("m", 2, d), dst=M2.at[d - 1])

    def mid_receive(p):
        buf = (M0, M1, M2)[p]
        for d in (1, 2, 3):
            arrive(buf.at[d - 1], sib, ("m", p, d))
        home = (G.at[0, :, y, :, x], G.at[1, :, y, :, x], G.at[2, zl, :, zh, x])[p]
        add(home, [buf.at[d] for d in range(3)])

    for p in (0, 1):
        for d in (1, 2, 3):
            mid_send(p, d)
    both("z", 5)
    both("z", 6)
    for d in (1, 2, 3):
        mid_send(2, d)
    jobs.pop(0)()

    def last_send(p, d):
        if p < 2:
            zz = (z + d) % 8
            start(G.at[p, zz % 2, y, zz // 2, x], at(dz=d), ("l", p, d), dst=(L0, L1)[p].at[d - 1])
        else:
            start(G.at[2, zl, (y + d) % 4, zh, x], at(dy=d), ("l", 2, d), dst=L2.at[d - 1])

    def last_receive(p):
        buf, n = ((L0, 7), (L1, 7), (L2, 3))[p]
        for d in range(n):
            arrive(buf.at[d], sib, ("l", p, d + 1))
        total = G[p, zl, y, zh, x].astype(F32)
        for d in range(n):
            total = total + buf[d].astype(F32)
        grad_ref[p] = total * (1.0 / 16.0)

    for p in (0, 1):
        mid_receive(p)
        for d in range(1, 8):
            last_send(p, d)
    mid_receive(2)
    for d in (1, 2, 3):
        last_send(2, d)
    while jobs:
        jobs.pop(0)()
    for p in range(3):
        last_receive(p)
    copies.of(W.at[:, :, c], W.at[:, :, c], sib, ("s",)).wait_send()
    copies.finish()
    out.wait()
    assert len(copies.ids) == N_COPIES, len(copies.ids)


def finish_kernel(pred_ref, ig_ref, grad_ref, pred_out, ig_out, conv_out, mix_out, sems):
    jobs = [pltpu.make_async_copy(ig_ref, ig_out, sems.at[4])]
    for i in range(4):
        rows = pl.ds(32 * i, 32)
        jobs.append(pltpu.make_async_copy(pred_ref.at[rows], pred_out.at[rows], sems.at[i]))
    for job in jobs:
        job.start()
    packed = jnp.concatenate([grad_ref[p] for p in range(3)], axis=1)
    for k in range(3):
        conv_out[k] = packed[:, 96 * k : 96 * k + 96]
    mix_out[...] = packed[:, 288:384]
    for job in jobs:
        job.wait()


def body(tower_input, norm_gain, conv_weight, mix_weight, head_weight, head_bias, pred_cotangent):
    vmem = pl.BlockSpec(memory_space=pltpu.VMEM)
    hbm = pl.BlockSpec(memory_space=pl.ANY)
    scratch = [
        ((6, 4, 2, 4, 4, 48, 128), BF16),
        ((2, 4, 2, CH, 256), BF16),
        ((BINS + 16, CH), F32),
        ((2, 8, BINS, 384), BF16),
        ((8, BINS, 384), BF16),
        ((BINS, INNER), F32),
        ((BINS, INNER), BF16),
        ((BINS, CH), BF16),
        ((BINS, CH), F32),
        ((2, 8, BINS, 128), BF16),
        ((8, BINS, 128), BF16),
        ((BINS + 16, INNER), F32),
        ((BINS + 16, INNER), BF16),
        ((INNER, 256), BF16),
        ((INNER, 256), BF16),
        ((3, BINS, INNER), BF16),
        ((BINS, CH), F32),
        ((BINS, TRACKS), BF16),
        ((3, 2, 4, 4, 4, 48, 128), BF16),
        ((2, 3, 4, 4, 48, 128), BF16),
        ((2, 3, 4, 4, 48, 128), BF16),
        ((2, 7, 2, 4, 48, 128), BF16),
        ((3, 2, 4, 48, 128), BF16),
        ((3, 2, 4, 48, 128), BF16),
        ((3, 4, 48, 128), BF16),
        ((7, 48, 128), BF16),
        ((7, 48, 128), BF16),
        ((3, 48, 128), BF16),
        ((BINS, INNER), F32),
    ]
    predictions, input_grad, grads = pl.pallas_call(
        kernel,
        out_shape=[
            jax.ShapeDtypeStruct((BINS, TRACKS), BF16),
            jax.ShapeDtypeStruct((BINS, CH), BF16),
            jax.ShapeDtypeStruct((3, 48, 128), F32),
        ],
        in_specs=[vmem, vmem, hbm, vmem, vmem, vmem, vmem],
        out_specs=[hbm, vmem, vmem],
        scratch_shapes=[pltpu.VMEM(*spec) for spec in scratch]
        + [
            pltpu.SemaphoreType.DMA((N_COPIES,)),
            pltpu.SemaphoreType.DMA((N_COPIES,)),
            pltpu.SemaphoreType.DMA((2,)),
        ],
        compiler_params=pltpu.CompilerParams(
            collective_id=0, has_side_effects=True, vmem_limit_bytes=60 * 2**20
        ),
        name="block",
    )(
        conv_weight.transpose(0, 2, 1),
        mix_weight,
        head_weight,
        tower_input[0],
        norm_gain,
        head_bias,
        pred_cotangent[0],
    )
    predictions, input_grad, conv_grad, mix_grad = pl.pallas_call(
        finish_kernel,
        out_shape=[
            jax.ShapeDtypeStruct((BINS, TRACKS), BF16),
            jax.ShapeDtypeStruct((BINS, CH), BF16),
            jax.ShapeDtypeStruct((3, 48, 96), F32),
            jax.ShapeDtypeStruct((48, 96), F32),
        ],
        in_specs=[vmem, vmem, vmem],
        out_specs=[hbm, hbm, vmem, vmem],
        scratch_shapes=[pltpu.SemaphoreType.DMA((5,))],
        name="unpack",
    )(predictions, input_grad, grads)
    return (predictions[None], input_grad[None], conv_grad.transpose(0, 2, 1), mix_grad)


def solution(mesh):
    in_specs = (
        P("batch", "seq", None),
        P(),
        P(None, "seq", "batch"),
        P("batch", "seq"),
        P(None, "seq"),
        P(),
        P("batch", "seq", None),
    )
    out_specs = (
        P("batch", "seq", None),
        P("batch", "seq", None),
        P(None, "seq", "batch"),
        P("batch", "seq"),
    )
    return jax.shard_map(body, mesh=mesh, in_specs=in_specs, out_specs=out_specs, check_vma=False)
```

```python
import functools

import jax
import jax.numpy as jnp
from jax import lax
from jax.experimental import pallas as pl
from jax.experimental.pallas import tpu as pltpu
from jax.sharding import PartitionSpec as P

CH = 1536
INNER = 768
TRACKS = 4096
STEP = 8
BINS = 128
BF16 = jnp.bfloat16
F32 = jnp.float32
ROOT = 0.7978845608028654
CUBE = 0.044715
LAST = (((1,), (1,)), ((), ()))
N_COPIES = 137


def place():
    b, s = lax.axis_index("batch"), lax.axis_index("seq")
    return b % 4, (s // 2) % 4, (b // 4) * 2 + s // 8, s % 2


def device(x, y, z, c):
    return ((z // 2) * 4 + x, (z % 2) * 8 + y * 2 + c)


class Copies:
    def __init__(self, send, recv):
        self.send, self.recv, self.sent, self.ids = send, recv, [], {}

    def of(self, src, dst, to, key):
        i = self.ids.setdefault(key, len(self.ids))
        return pltpu.make_async_remote_copy(
            src_ref=src,
            dst_ref=dst,
            send_sem=self.send.at[i],
            recv_sem=self.recv.at[i],
            device_id=to,
            device_id_type=pl.DeviceIdType.MESH,
        )

    def start(self, block, to, key, dst=None):
        copy = self.of(block, block if dst is None else dst, to, key)
        copy.start()
        self.sent.append(copy)

    def arrive(self, block, to, key):
        self.of(block, block, to, key).wait_recv()

    def group(self, block, to, key):
        self.of(block, block, to, key).start()

    def finish(self):
        for copy in self.sent:
            copy.wait_send()


def meet(x, y, z, c):
    b, s = lax.axis_index("batch"), lax.axis_index("seq")
    others = [device(x, y, z, 1 - c), (b, (s + 1) % 16), (b, (s + 15) % 16)]
    others += [device((x + d) % 4, y, z, c) for d in (1, 2, 3)]
    others += [device(x, (y + d) % 4, z, c) for d in (1, 2, 3)]
    others += [device(x, y, (z + d) % 8, c) for d in range(1, 8)]
    barrier = pltpu.get_barrier_semaphore()
    for other in others:
        pl.semaphore_signal(barrier, inc=1, device_id=other, device_id_type=pl.DeviceIdType.MESH)
    pl.semaphore_wait(barrier, len(others))


def gelu(v):
    return 0.5 * v * (1.0 + jnp.tanh(ROOT * (v + CUBE * v * v * v)))


def gelu_slope(v):
    t = jnp.tanh(ROOT * (v + CUBE * v * v * v))
    return 0.5 * (1.0 + t) + 0.5 * v * (1.0 - t * t) * (ROOT * (1.0 + 3.0 * CUBE * v * v))


def rows_loop(total, step):
    def run(body):
        def one(i, carry):
            body(pl.multiple_of(i * step, step))
            return carry

        lax.fori_loop(0, total // step, one, 0)

    return run


def kernel(
    taps_ref, mix_ref, h_ref, in_ref, gain_ref, bias_ref, cot_in,
    pred_out, ig_ref, grad_ref,
    W, H, act, AP, AX, conv, hidden, tower, dtower, DT, DX, dext, dext16, hT, dT, dh2, dact,
    pred_ref, cot_ref, G, RX, RY, RZ, M0, M1, M2, L0, L1, L2, sum0,
    send, recv, local,
):
    x, y, z, c = place()
    b, s = lax.axis_index("batch"), lax.axis_index("seq")
    zl, zh = z % 2, z // 2
    sib = device(x, y, z, 1 - c)
    before, after = (b, (s + 15) % 16), (b, (s + 1) % 16)
    own = pltpu.make_async_copy(h_ref, H.at[zl, y, c], local.at[0])
    own.start()
    cot_copy = pltpu.make_async_copy(cot_in, cot_ref, local.at[2])
    cot_copy.start()
    packed = [taps_ref[k].astype(F32) for k in range(3)] + [mix_ref[...].astype(F32)]
    packed = jnp.concatenate(packed, axis=1).astype(BF16)
    for p in range(3):
        t = 3 * zl + p if p < 2 else 5 - 3 * zl
        W[t, y, c, zh, x] = packed[:, 128 * p : 128 * p + 128]
    meet(x, y, z, c)
    copies = Copies(send, recv)
    start, arrive = copies.start, copies.arrive

    def at(dx=0, dy=0, dz=0):
        return device((x + dx) % 4, (y + dy) % 4, (z + dz) % 8, c)

    def shard(part, dz):
        zz = (z + dz) % 8
        t = pl.ds(3 * (zz % 2), 2) if part == 0 else pl.ds(5 - 3 * (zz % 2), 1)
        return W.at[t, y, c, zz // 2, x]

    def col(part, dx, dy, core=c):
        t = pl.ds(0, 5) if part == 0 else pl.ds(5, 1)
        return W.at[t, (y + dy) % 4, core, :, (x + dx) % 4]

    def half_col(part, dx, dy, half):
        if part == 0:
            cut = 3 if dy in (0, 1) else 2
            t = pl.ds(0, cut) if half == 0 else pl.ds(cut, 5 - cut)
            return W.at[t, (y + dy) % 4, c, :, (x + dx) % 4]
        return W.at[5, (y + dy) % 4, c, pl.ds(2 * half, 2), (x + dx) % 4]

    def mid_half(part, at_d, d):
        zhs = pl.ds(0, 2) if d == 1 else pl.ds(2, 2)
        if part == 0:
            return W.at[pl.ds(0, 5), (y + at_d) % 4, c, zhs, x]
        return W.at[5, y, c, zhs, (x + at_d) % 4]

    def head(dzl, dy, half):
        rows = slice(None) if half is None else pl.ds(half * 768, 768)
        return H.at[(zl + dzl) % 2, (y + dy) % 4, c, rows]

    def spread(d):
        start(col(0, 0, d), at(dx=1), ("p3", 0, 1, d % 4))
        start(col(0, 0, d), at(dx=-1), ("p3", 0, 3, d % 4))
        start(col(1, d, 0), at(dy=1), ("p3", 1, 1, d % 4))
        start(col(1, d, 0), at(dy=-1), ("p3", 1, 3, d % 4))
        copies.group(col(0, 0, d), sib, ("s",))
        copies.group(col(1, d, 0), sib, ("s",))

    def second_hop(q):
        for d in (1, -1):
            half = 0 if d == 1 else 1
            arrive(col(0, -d, q), sib, ("p3", 0, d % 4, q % 4))
            start(half_col(0, -d, q, half), at(dx=d), ("p4", 0, d % 4, q % 4))
            copies.group(col(0, -d, q), sib, ("s",))
            arrive(col(1, q, -d), sib, ("p3", 1, d % 4, q % 4))
            start(half_col(1, q, -d, half), at(dy=d), ("p4", 1, d % 4, q % 4))
            copies.group(col(1, q, -d), sib, ("s",))

    def last_hop(q):
        for half, d in ((0, 1), (1, -1)):
            arrive(half_col(0, 2, q, half), sib, ("p4", 0, d % 4, q % 4))
            arrive(half_col(1, q, 2, half), sib, ("p4", 1, d % 4, q % 4))
        copies.group(col(0, 2, q), sib, ("s",))
        copies.group(col(1, q, 2), sib, ("s",))

    def head_own(first):
        for d, half in ((1, 0), (-1, 1)):
            half = half if first else 1 - half
            start(head(0, 0, half), at(dy=d), ("hy", d % 4, half))

    def head_first():
        for d, half in ((1, 0), (-1, 1)):
            arrive(head(0, -d, half), sib, ("hy", d % 4, half))
            start(head(0, -d, half), at(dz=d), ("hz", d % 8, -d % 4))

    def head_on():
        for d, half in ((1, 0), (-1, 1)):
            start(head(0, -d, half), at(dy=d), ("hy2", d % 4))

    def head_second():
        for d, half in ((1, 0), (-1, 1)):
            arrive(head(0, -d, 1 - half), sib, ("hy", d % 4, 1 - half))
            start(head(0, -d, 1 - half), at(dz=-d), ("hz", -d % 8, -d % 4))
            start(head(0, -d, None), sib, ("hs", 0, -d % 4))

    def head_third():
        arrive(head(0, 2, 0), sib, ("hy2", 1))
        start(head(0, 2, 0), at(dz=1), ("hz", 1, 2))
        arrive(head(0, 2, 1), sib, ("hy2", 3))
        start(head(0, 2, 1), at(dz=-1), ("hz", 7, 2))
        start(head(0, 2, None), sib, ("hs", 0, 2))

    def head_other(dy):
        arrive(head(1, dy, 0), sib, ("hz", 1, dy % 4))
        arrive(head(1, dy, 1), sib, ("hz", 7, dy % 4))
        start(head(1, dy, None), sib, ("hs", 1, dy % 4))

    def from_sib():
        arrive(W.at[:, :, 1 - c], sib, ("s",))

    for dz in (1, -1, 2, -2, 3, -3, 4):
        start(shard(0, 0), at(dz=dz), ("z", 0, dz % 8))
        start(shard(1, 0), at(dz=dz), ("z", 1, dz % 8))
    own.wait()
    head_own(True)
    start(head(0, 0, None), sib, ("hs", 0, 0))

    @rows_loop(BINS, 16)
    def _(r):
        v = in_ref[pl.ds(r, 16), :].astype(F32)
        mean_sq = jnp.mean(v * v, axis=-1, keepdims=True)
        a = gelu(v * lax.rsqrt(mean_sq + 1e-06) * gain_ref[...].reshape(1, CH))
        act[pl.ds(r + 8, 16), :] = a.astype(BF16).astype(F32)

    start(act.at[pl.ds(8, 8)], before, ("halo", 0), dst=act.at[pl.ds(136, 8)])
    start(act.at[pl.ds(128, 8)], after, ("halo", 1), dst=act.at[pl.ds(0, 8)])

    for dz in (1, -1, 2, -2, 3, -3, 4):
        arrive(shard(0, -dz), sib, ("z", 0, dz % 8))
        arrive(shard(1, -dz), sib, ("z", 1, dz % 8))
    for d in (1, -1):
        start(col(0, 0, 0), at(dy=d), ("p2", 0, d % 4))
        start(col(1, 0, 0), at(dx=d), ("p2", 1, d % 4))
    spread(0)
    start(head(0, 0, 0), at(dz=1), ("hz", 1, 0))
    start(head(0, 0, 1), at(dz=-1), ("hz", 7, 0))
    head_first()
    for d in (1, -1):
        arrive(col(0, 0, -d), sib, ("p2", 0, d % 4))
        start(mid_half(0, -d, d), at(dy=d), ("p2r", 0, d % 4))
        arrive(col(1, -d, 0), sib, ("p2", 1, d % 4))
        start(mid_half(1, -d, d), at(dx=d), ("p2r", 1, d % 4))
        spread(-d)
    second_hop(0)
    head_own(False)
    arrive(act.at[pl.ds(136, 8)], sib, ("halo", 0))
    arrive(act.at[pl.ds(0, 8)], sib, ("halo", 1))

    @pl.when(s == 0)
    def _():
        act[0:8, :] = jnp.zeros((8, CH), F32)

    @pl.when(s == 15)
    def _():
        act[136:144, :] = jnp.zeros((8, CH), F32)

    for d in (1, -1):
        arrive(mid_half(0, 2, d), sib, ("p2r", 0, d % 4))
        arrive(mid_half(1, 2, d), sib, ("p2r", 1, d % 4))
    spread(2)
    head_on()

    @rows_loop(BINS, 16)
    def _(r):
        for q in range(4):
            taps = [act[pl.ds(r + 8 * k, 16), pl.ds(q * 384, 384)] for k in range(3)]
            for i in range(4):
                g = 4 * q + i
                pieces = [t[:, 96 * i : 96 * i + 96] for t in taps] + [jnp.zeros((16, 96), F32)]
                AP[g % 2, g // 2, pl.ds(r, 16), :] = jnp.concatenate(pieces, axis=1).astype(BF16)

    start(AP.at[1 - c], sib, ("ax",), dst=AX)
    last_hop(0)
    head_second()
    second_hop(-1)
    second_hop(1)
    second_hop(2)
    head_third()
    last_hop(-1)
    last_hop(1)
    last_hop(2)
    from_sib()

    def w(p, j, cc):
        t = 3 * (j // 4) + p if p < 2 else 5 - 3 * (j // 4)
        return W[t, j % 4, cc].reshape(INNER, 128)

    conv[...] = jnp.zeros_like(conv)

    def conv_step(j, carry):
        lhs = jnp.concatenate([AP[0, j], AP[1, j]], axis=1)
        rhs = jnp.concatenate([w(p, j, cc) for cc in range(2) for p in range(3)], axis=1)
        conv[...] += lax.dot_general(lhs, rhs, LAST, preferred_element_type=F32)
        return carry

    lax.fori_loop(0, 8, conv_step, 0)
    for dy in (0, -1, 1):
        head_other(dy)

    @rows_loop(BINS, 16)
    def _(r):
        hidden[pl.ds(r, 16), :] = gelu(conv[pl.ds(r, 16), :]).astype(BF16)

    start(hidden, sib, ("hidden",), dst=dh2.at[0])

    for q in range(4):
        mixed = []
        for i in range(2):
            j = 2 * q + i
            rhs = jnp.concatenate([w(2, j, 0), w(2, j, 1)], axis=1)
            m = jnp.dot(hidden[...], rhs, preferred_element_type=F32)
            mixed += [m[:, 32:128], m[:, 160:256]]
        lanes = slice(384 * q, 384 * q + 384)
        tower[:, lanes] = (in_ref[:, lanes].astype(F32) + jnp.concatenate(mixed, axis=1)).astype(BF16)

    dtower[...] = jnp.zeros_like(dtower)
    cot_copy.wait()

    def head_step(zz, yy):
        lanes = pl.ds(pl.multiple_of((zz * 4 + yy) * 512, 512), 512)
        weight = jnp.concatenate([H[zz, yy, 0], H[zz, yy, 1]], axis=1)
        logits = jnp.dot(tower[...], weight, preferred_element_type=F32) + bias_ref[lanes].reshape(1, -1)
        e = jnp.exp(-jnp.abs(logits))
        pred_ref[:, lanes] = (jnp.maximum(logits, 0.0) + jnp.log1p(e)).astype(BF16)
        sigmoid = jnp.where(logits >= 0.0, 1.0, e) / (1.0 + e)
        dlogits = (cot_ref[:, lanes].astype(F32) * sigmoid).astype(BF16)
        dtower[...] += lax.dot_general(dlogits, weight, LAST, preferred_element_type=F32)

    def ready(dzl, dy):
        arrive(H.at[(zl + dzl) % 2, (y + dy) % 4, 1 - c], sib, ("hs", dzl, dy % 4))

    for dzl in (0, 1):
        for dy in (0, -1, 1, 2):
            ready(dzl, dy)
            head_step((zl + dzl) % 2, (y + dy) % 4)
            if dzl == 0 and dy == -1:
                head_other(2)
    out = pltpu.make_async_copy(pred_ref, pred_out, local.at[1])
    out.start()

    @rows_loop(BINS, 16)
    def _(r):
        for q in range(4):
            v = dtower[pl.ds(r, 16), pl.ds(q * 384, 384)]
            for i in range(4):
                g = 4 * q + i
                pieces = [jnp.zeros((16, 32), F32), v[:, 96 * i : 96 * i + 96]]
                DT[g % 2, g // 2, pl.ds(r, 16), :] = jnp.concatenate(pieces, axis=1).astype(BF16)

    start(DT.at[1 - c], sib, ("dt",), dst=DX)
    sum0[...] = jnp.zeros_like(sum0)

    def dhidden_step(j, carry):
        lhs = jnp.concatenate([DT[0, j], DT[1, j]], axis=1)
        rhs = jnp.concatenate([w(2, j, 0), w(2, j, 1)], axis=1)
        sum0[...] += lax.dot_general(lhs, rhs, LAST, preferred_element_type=F32)
        return carry

    lax.fori_loop(0, 8, dhidden_step, 0)

    @rows_loop(BINS, 16)
    def _(r):
        d = sum0[pl.ds(r, 16), :] * gelu_slope(conv[pl.ds(r, 16), :])
        half = d.astype(BF16)
        dh2[2, pl.ds(r, 16), :] = half
        dext[pl.ds(r + 8, 16), :] = half.astype(F32)

    start(dh2.at[2], sib, ("dconv",), dst=dh2.at[1])
    start(dext.at[pl.ds(8, 8)], before, ("dhalo", 0), dst=dext.at[pl.ds(136, 8)])
    start(dext.at[pl.ds(128, 8)], after, ("dhalo", 1), dst=dext.at[pl.ds(0, 8)])

    arrive(dh2.at[0], sib, ("hidden",))
    hT[:, 0:128] = hidden[...].T
    hT[:, 128:256] = dh2[0].T
    dT[:, 0:128] = dh2[2].T
    arrive(AX, sib, ("ax",))
    arrive(DX, sib, ("dt",))
    arrive(dh2.at[1], sib, ("dconv",))
    dT[:, 128:256] = dh2[1].T

    def grad_step(j, carry):
        rhs = jnp.concatenate([AP[c, j], AX[j]], axis=0)
        g = jnp.dot(dT[...], rhs, preferred_element_type=F32)
        more = jnp.dot(hT[...], jnp.concatenate([DT[c, j], DX[j]], axis=0), preferred_element_type=F32)
        for p in range(3):
            part = g[:, 128 * p : 128 * p + 128]
            if p == 2:
                part = part + more
            G[p, j // 4, j % 4] = part.astype(BF16).reshape(4, 4, 48, 128)
        return carry

    lax.fori_loop(0, 8, grad_step, 0)

    def dact_prepare():
        arrive(dext.at[pl.ds(136, 8)], sib, ("dhalo", 0))
        arrive(dext.at[pl.ds(0, 8)], sib, ("dhalo", 1))

        @pl.when(s == 0)
        def _():
            dext[0:8, :] = jnp.zeros((8, INNER), F32)

        @pl.when(s == 15)
        def _():
            dext[136:144, :] = jnp.zeros((8, INNER), F32)

        dext16[...] = dext[...].astype(BF16)

    def dact_part(q):
        pieces = []
        for i in range(2):
            j = 2 * q + i
            for cc in range(2):
                rhs = jnp.concatenate([w(p, j, cc) for p in range(3)], axis=1)
                d = jnp.dot(dext16[...], rhs, preferred_element_type=F32)
                pieces.append(d[16:144, 0:96] + d[8:136, 96:192] + d[0:128, 192:288])
        dact[:, 384 * q : 384 * q + 384] = jnp.concatenate(pieces, axis=1)

    def dact_finish():
        @rows_loop(BINS, 16)
        def _(r):
            v = in_ref[pl.ds(r, 16), :].astype(F32)
            rs = lax.rsqrt(jnp.mean(v * v, axis=-1, keepdims=True) + 1e-06)
            gain = gain_ref[...].reshape(1, CH)
            dz = dact[pl.ds(r, 16), :] * gelu_slope(v * rs * gain) * gain
            dot = jnp.mean(dz * v, axis=-1, keepdims=True)
            ig = dtower[pl.ds(r, 16), :] + dz * rs - v * (rs * rs * rs * dot)
            ig_ref[pl.ds(r, 16), :] = ig.astype(BF16)

    jobs = [dact_prepare] + [functools.partial(dact_part, q) for q in range(4)] + [dact_finish]

    def half_x(m, h):
        return G.at[0, h, :, :, (x + m) % 4]

    def half_y(m, h):
        return G.at[1, h, (y + m) % 4]

    def half_z(m, h):
        zz = (z + m) % 8
        return G.at[2, zz % 2, pl.ds(2 * h, 2), zz // 2]

    def slots(ring):
        return [(0, m) for m in range(ring, 0, -1)], [(1, m) for m in range(ring - 1, 0, -1)]

    def order(n):
        seq = []
        for m in range(n // 2, 0, -1):
            seq.append((0, m))
            if m > 1:
                seq.append((1, m - 1))
        return seq

    rings = {"x": (4, half_x, RX, "dx"), "y": (4, half_y, RY, "dy"), "z": (8, half_z, RZ, "dz")}

    def ring_send(ax, d, k):
        n, block, buf, name = rings[ax]
        h, m = order(n)[k]
        h = h if d < 0 else 1 - h
        start(block(d * m, h), at(**{name: d}), ("r" + ax, d, k), dst=buf.at[(d + 1) // 2, k])

    def add(dst, srcs):
        total = dst[...].astype(F32)
        for src in srcs:
            total = total + src[...].astype(F32)
        dst[...] = total.astype(BF16)

    def ring_receive(ax, d, k):
        n, block, buf, name = rings[ax]
        seq = order(n)
        h, m = seq[k]
        slot = buf.at[(d + 1) // 2, k]
        arrive(slot, sib, ("r" + ax, d, k))
        mine = h if d < 0 else 1 - h
        add(block(d * (m - 1), mine), [slot])
        if m > 1:
            ring_send(ax, d, seq.index((h, m - 1)))

    for ax in "xyz":
        for d in (-1, 1):
            ring_send(ax, d, 0)
            ring_send(ax, d, 1)
    jobs.pop(0)()
    jobs.pop(0)()

    def both(ax, k):
        for d in (-1, 1):
            ring_receive(ax, d, k)

    both("z", 0)
    both("x", 0)
    both("y", 0)
    both("z", 1)
    jobs.pop(0)()
    both("z", 2)
    both("x", 1)
    both("y", 1)
    both("z", 3)
    jobs.pop(0)()
    both("z", 4)
    both("x", 2)
    both("y", 2)

    def mid_send(p, d):
        if p == 0:
            start(G.at[0, :, (y + d) % 4, :, x], at(dy=d), ("m", 0, d), dst=M0.at[d - 1])
        elif p == 1:
            start(G.at[1, :, y, :, (x + d) % 4], at(dx=d), ("m", 1, d), dst=M1.at[d - 1])
        else:
            start(G.at[2, zl, :, zh, (x + d) % 4], at(dx=d), ("m", 2, d), dst=M2.at[d - 1])

    def mid_receive(p):
        buf = (M0, M1, M2)[p]
        for d in (1, 2, 3):
            arrive(buf.at[d - 1], sib, ("m", p, d))
        home = (G.at[0, :, y, :, x], G.at[1, :, y, :, x], G.at[2, zl, :, zh, x])[p]
        add(home, [buf.at[d] for d in range(3)])

    for p in (0, 1):
        for d in (1, 2, 3):
            mid_send(p, d)
    both("z", 5)
    both("z", 6)
    for d in (1, 2, 3):
        mid_send(2, d)
    jobs.pop(0)()

    def last_send(p, d):
        if p < 2:
            zz = (z + d) % 8
            start(G.at[p, zz % 2, y, zz // 2, x], at(dz=d), ("l", p, d), dst=(L0, L1)[p].at[d - 1])
        else:
            start(G.at[2, zl, (y + d) % 4, zh, x], at(dy=d), ("l", 2, d), dst=L2.at[d - 1])

    def last_receive(p):
        buf, n = ((L0, 7), (L1, 7), (L2, 3))[p]
        for d in range(n):
            arrive(buf.at[d], sib, ("l", p, d + 1))
        total = G[p, zl, y, zh, x].astype(F32)
        for d in range(n):
            total = total + buf[d].astype(F32)
        grad_ref[p] = total * (1.0 / 16.0)

    for p in (0, 1):
        mid_receive(p)
        for d in range(1, 8):
            last_send(p, d)
    mid_receive(2)
    for d in (1, 2, 3):
        last_send(2, d)
    while jobs:
        jobs.pop(0)()
    for p in range(3):
        last_receive(p)
    copies.of(W.at[:, :, c], W.at[:, :, c], sib, ("s",)).wait_send()
    copies.finish()
    out.wait()
    assert len(copies.ids) == N_COPIES, len(copies.ids)


def finish_kernel(pred_ref, ig_ref, grad_ref, pred_out, ig_out, conv_out, mix_out):
    pred_out[...] = pred_ref[...]
    ig_out[...] = ig_ref[...]

    @pl.when(pl.program_id(0) == 0)
    def _():
        packed = jnp.concatenate([grad_ref[p] for p in range(3)], axis=1)
        for k in range(3):
            conv_out[k] = packed[:, 96 * k : 96 * k + 96]
        mix_out[...] = packed[:, 288:384]


def body(tower_input, norm_gain, conv_weight, mix_weight, head_weight, head_bias, pred_cotangent):
    vmem = pl.BlockSpec(memory_space=pltpu.VMEM)
    hbm = pl.BlockSpec(memory_space=pl.ANY)
    scratch = [
        ((6, 4, 2, 4, 4, 48, 128), BF16),
        ((2, 4, 2, CH, 256), BF16),
        ((BINS + 16, CH), F32),
        ((2, 8, BINS, 384), BF16),
        ((8, BINS, 384), BF16),
        ((BINS, INNER), F32),
        ((BINS, INNER), BF16),
        ((BINS, CH), BF16),
        ((BINS, CH), F32),
        ((2, 8, BINS, 128), BF16),
        ((8, BINS, 128), BF16),
        ((BINS + 16, INNER), F32),
        ((BINS + 16, INNER), BF16),
        ((INNER, 256), BF16),
        ((INNER, 256), BF16),
        ((3, BINS, INNER), BF16),
        ((BINS, CH), F32),
        ((BINS, TRACKS), BF16),
        ((BINS, TRACKS), BF16),
        ((3, 2, 4, 4, 4, 48, 128), BF16),
        ((2, 3, 4, 4, 48, 128), BF16),
        ((2, 3, 4, 4, 48, 128), BF16),
        ((2, 7, 2, 4, 48, 128), BF16),
        ((3, 2, 4, 48, 128), BF16),
        ((3, 2, 4, 48, 128), BF16),
        ((3, 4, 48, 128), BF16),
        ((7, 48, 128), BF16),
        ((7, 48, 128), BF16),
        ((3, 48, 128), BF16),
        ((BINS, INNER), F32),
    ]
    predictions, input_grad, grads = pl.pallas_call(
        kernel,
        out_shape=[
            jax.ShapeDtypeStruct((BINS, TRACKS), BF16),
            jax.ShapeDtypeStruct((BINS, CH), BF16),
            jax.ShapeDtypeStruct((3, 48, 128), F32),
        ],
        in_specs=[vmem, vmem, hbm, vmem, vmem, vmem, hbm],
        out_specs=[hbm, vmem, vmem],
        scratch_shapes=[pltpu.VMEM(*spec) for spec in scratch]
        + [
            pltpu.SemaphoreType.DMA((N_COPIES,)),
            pltpu.SemaphoreType.DMA((N_COPIES,)),
            pltpu.SemaphoreType.DMA((3,)),
        ],
        compiler_params=pltpu.CompilerParams(
            collective_id=0, has_side_effects=True, vmem_limit_bytes=60 * 2**20
        ),
        name="block",
    )(
        conv_weight.transpose(0, 2, 1),
        mix_weight,
        head_weight,
        tower_input[0],
        norm_gain,
        head_bias,
        pred_cotangent[0],
    )
    predictions, input_grad, conv_grad, mix_grad = pl.pallas_call(
        finish_kernel,
        out_shape=[
            jax.ShapeDtypeStruct((BINS, TRACKS), BF16),
            jax.ShapeDtypeStruct((BINS, CH), BF16),
            jax.ShapeDtypeStruct((3, 48, 96), F32),
            jax.ShapeDtypeStruct((48, 96), F32),
        ],
        grid=(4,),
        in_specs=[
            pl.BlockSpec((32, TRACKS), lambda i: (i, 0)),
            pl.BlockSpec((32, CH), lambda i: (i, 0)),
            pl.BlockSpec((3, 48, 128), lambda i: (0, 0, 0)),
        ],
        out_specs=[
            pl.BlockSpec((32, TRACKS), lambda i: (i, 0)),
            pl.BlockSpec((32, CH), lambda i: (i, 0)),
            pl.BlockSpec((3, 48, 96), lambda i: (0, 0, 0)),
            pl.BlockSpec((48, 96), lambda i: (0, 0)),
        ],
        name="unpack",
    )(predictions, input_grad, grads)
    return (predictions[None], input_grad[None], conv_grad.transpose(0, 2, 1), mix_grad)


def solution(mesh):
    in_specs = (
        P("batch", "seq", None),
        P(),
        P(None, "seq", "batch"),
        P("batch", "seq"),
        P(None, "seq"),
        P(),
        P("batch", "seq", None),
    )
    out_specs = (
        P("batch", "seq", None),
        P("batch", "seq", None),
        P(None, "seq", "batch"),
        P("batch", "seq"),
    )
    return jax.shard_map(body, mesh=mesh, in_specs=in_specs, out_specs=out_specs, check_vma=False)
```

```python
import functools

import jax
import jax.numpy as jnp
from jax import lax
from jax.experimental import pallas as pl
from jax.experimental.pallas import tpu as pltpu
from jax.sharding import PartitionSpec as P

CH = 1536
INNER = 768
TRACKS = 4096
STEP = 8
BINS = 128
BF16 = jnp.bfloat16
F32 = jnp.float32
ROOT = 0.7978845608028654
CUBE = 0.044715
LAST = (((1,), (1,)), ((), ()))
N_COPIES = 137


def place():
    b, s = lax.axis_index("batch"), lax.axis_index("seq")
    return b % 4, (s // 2) % 4, (b // 4) * 2 + s // 8, s % 2


def device(x, y, z, c):
    return ((z // 2) * 4 + x, (z % 2) * 8 + y * 2 + c)


class Copies:
    def __init__(self, send, recv):
        self.send, self.recv, self.sent, self.ids = send, recv, [], {}

    def of(self, src, dst, to, key):
        i = self.ids.setdefault(key, len(self.ids))
        return pltpu.make_async_remote_copy(
            src_ref=src,
            dst_ref=dst,
            send_sem=self.send.at[i],
            recv_sem=self.recv.at[i],
            device_id=to,
            device_id_type=pl.DeviceIdType.MESH,
        )

    def start(self, block, to, key, dst=None):
        copy = self.of(block, block if dst is None else dst, to, key)
        copy.start()
        self.sent.append(copy)

    def arrive(self, block, to, key):
        self.of(block, block, to, key).wait_recv()

    def group(self, block, to, key):
        self.of(block, block, to, key).start()

    def finish(self):
        for copy in self.sent:
            copy.wait_send()


def meet(x, y, z, c):
    b, s = lax.axis_index("batch"), lax.axis_index("seq")
    others = [device(x, y, z, 1 - c), (b, (s + 1) % 16), (b, (s + 15) % 16)]
    others += [device((x + d) % 4, y, z, c) for d in (1, 2, 3)]
    others += [device(x, (y + d) % 4, z, c) for d in (1, 2, 3)]
    others += [device(x, y, (z + d) % 8, c) for d in range(1, 8)]
    barrier = pltpu.get_barrier_semaphore()
    for other in others:
        pl.semaphore_signal(barrier, inc=1, device_id=other, device_id_type=pl.DeviceIdType.MESH)
    pl.semaphore_wait(barrier, len(others))


def gelu(v):
    return 0.5 * v * (1.0 + jnp.tanh(ROOT * (v + CUBE * v * v * v)))


def gelu_slope(v):
    t = jnp.tanh(ROOT * (v + CUBE * v * v * v))
    return 0.5 * (1.0 + t) + 0.5 * v * (1.0 - t * t) * (ROOT * (1.0 + 3.0 * CUBE * v * v))


def rows_loop(total, step):
    def run(body):
        def one(i, carry):
            body(pl.multiple_of(i * step, step))
            return carry

        lax.fori_loop(0, total // step, one, 0)

    return run


def kernel(
    taps_ref, mix_ref, h_ref, in_ref, gain_ref, bias_ref, cot_in,
    pred_out, ig_ref, grad_ref,
    W, H, act, AP, AX, conv, hidden, tower, dtower, DT, DX, dext, dext16, hT, dT, dh2, dact,
    pred_ref, cot_ref, G, RX, RY, RZ, M0, M1, M2, L0, L1, L2, sum0,
    send, recv, local,
):
    x, y, z, c = place()
    b, s = lax.axis_index("batch"), lax.axis_index("seq")
    zl, zh = z % 2, z // 2
    sib = device(x, y, z, 1 - c)
    before, after = (b, (s + 15) % 16), (b, (s + 1) % 16)
    own = pltpu.make_async_copy(h_ref, H.at[zl, y, c], local.at[0])
    own.start()
    cot_copy = pltpu.make_async_copy(cot_in, cot_ref, local.at[2])
    cot_copy.start()
    packed = [taps_ref[k].astype(F32) for k in range(3)] + [mix_ref[...].astype(F32)]
    packed = jnp.concatenate(packed, axis=1).astype(BF16)
    for p in range(3):
        t = 3 * zl + p if p < 2 else 5 - 3 * zl
        W[t, y, c, zh, x] = packed[:, 128 * p : 128 * p + 128]
    meet(x, y, z, c)
    copies = Copies(send, recv)
    start, arrive = copies.start, copies.arrive

    def at(dx=0, dy=0, dz=0):
        return device((x + dx) % 4, (y + dy) % 4, (z + dz) % 8, c)

    def shard(part, dz):
        zz = (z + dz) % 8
        t = pl.ds(3 * (zz % 2), 2) if part == 0 else pl.ds(5 - 3 * (zz % 2), 1)
        return W.at[t, y, c, zz // 2, x]

    def col(part, dx, dy, core=c):
        t = pl.ds(0, 5) if part == 0 else pl.ds(5, 1)
        return W.at[t, (y + dy) % 4, core, :, (x + dx) % 4]

    def half_col(part, dx, dy, half):
        if part == 0:
            cut = 3 if dy in (0, 1) else 2
            t = pl.ds(0, cut) if half == 0 else pl.ds(cut, 5 - cut)
            return W.at[t, (y + dy) % 4, c, :, (x + dx) % 4]
        return W.at[5, (y + dy) % 4, c, pl.ds(2 * half, 2), (x + dx) % 4]

    def mid_half(part, at_d, d):
        zhs = pl.ds(0, 2) if d == 1 else pl.ds(2, 2)
        if part == 0:
            return W.at[pl.ds(0, 5), (y + at_d) % 4, c, zhs, x]
        return W.at[5, y, c, zhs, (x + at_d) % 4]

    def head(dzl, dy, half):
        rows = slice(None) if half is None else pl.ds(half * 768, 768)
        return H.at[(zl + dzl) % 2, (y + dy) % 4, c, rows]

    def spread(d):
        start(col(0, 0, d), at(dx=1), ("p3", 0, 1, d % 4))
        start(col(0, 0, d), at(dx=-1), ("p3", 0, 3, d % 4))
        start(col(1, d, 0), at(dy=1), ("p3", 1, 1, d % 4))
        start(col(1, d, 0), at(dy=-1), ("p3", 1, 3, d % 4))
        copies.group(col(0, 0, d), sib, ("s",))
        copies.group(col(1, d, 0), sib, ("s",))

    def second_hop(q):
        for d in (1, -1):
            half = 0 if d == 1 else 1
            arrive(col(0, -d, q), sib, ("p3", 0, d % 4, q % 4))
            start(half_col(0, -d, q, half), at(dx=d), ("p4", 0, d % 4, q % 4))
            copies.group(col(0, -d, q), sib, ("s",))
            arrive(col(1, q, -d), sib, ("p3", 1, d % 4, q % 4))
            start(half_col(1, q, -d, half), at(dy=d), ("p4", 1, d % 4, q % 4))
            copies.group(col(1, q, -d), sib, ("s",))

    def last_hop(q):
        for half, d in ((0, 1), (1, -1)):
            arrive(half_col(0, 2, q, half), sib, ("p4", 0, d % 4, q % 4))
            arrive(half_col(1, q, 2, half), sib, ("p4", 1, d % 4, q % 4))
        copies.group(col(0, 2, q), sib, ("s",))
        copies.group(col(1, q, 2), sib, ("s",))

    def head_own(first):
        for d, half in ((1, 0), (-1, 1)):
            half = half if first else 1 - half
            start(head(0, 0, half), at(dy=d), ("hy", d % 4, half))

    def head_first():
        for d, half in ((1, 0), (-1, 1)):
            arrive(head(0, -d, half), sib, ("hy", d % 4, half))
            start(head(0, -d, half), at(dz=d), ("hz", d % 8, -d % 4))

    def head_on():
        for d, half in ((1, 0), (-1, 1)):
            start(head(0, -d, half), at(dy=d), ("hy2", d % 4))

    def head_second():
        for d, half in ((1, 0), (-1, 1)):
            arrive(head(0, -d, 1 - half), sib, ("hy", d % 4, 1 - half))
            start(head(0, -d, 1 - half), at(dz=-d), ("hz", -d % 8, -d % 4))
            start(head(0, -d, None), sib, ("hs", 0, -d % 4))

    def head_third():
        arrive(head(0, 2, 0), sib, ("hy2", 1))
        start(head(0, 2, 0), at(dz=1), ("hz", 1, 2))
        arrive(head(0, 2, 1), sib, ("hy2", 3))
        start(head(0, 2, 1), at(dz=-1), ("hz", 7, 2))
        start(head(0, 2, None), sib, ("hs", 0, 2))

    def head_other(dy):
        arrive(head(1, dy, 0), sib, ("hz", 1, dy % 4))
        arrive(head(1, dy, 1), sib, ("hz", 7, dy % 4))
        start(head(1, dy, None), sib, ("hs", 1, dy % 4))

    def from_sib():
        arrive(W.at[:, :, 1 - c], sib, ("s",))

    for dz in (1, -1, 2, -2, 3, -3, 4):
        start(shard(0, 0), at(dz=dz), ("z", 0, dz % 8))
        start(shard(1, 0), at(dz=dz), ("z", 1, dz % 8))
    own.wait()
    head_own(True)
    start(head(0, 0, None), sib, ("hs", 0, 0))

    @rows_loop(BINS, 16)
    def _(r):
        v = in_ref[pl.ds(r, 16), :].astype(F32)
        mean_sq = jnp.mean(v * v, axis=-1, keepdims=True)
        a = gelu(v * lax.rsqrt(mean_sq + 1e-06) * gain_ref[...].reshape(1, CH))
        act[pl.ds(r + 8, 16), :] = a.astype(BF16).astype(F32)

    start(act.at[pl.ds(8, 8)], before, ("halo", 0), dst=act.at[pl.ds(136, 8)])
    start(act.at[pl.ds(128, 8)], after, ("halo", 1), dst=act.at[pl.ds(0, 8)])

    for dz in (1, -1, 2, -2, 3, -3, 4):
        arrive(shard(0, -dz), sib, ("z", 0, dz % 8))
        arrive(shard(1, -dz), sib, ("z", 1, dz % 8))
    for d in (1, -1):
        start(col(0, 0, 0), at(dy=d), ("p2", 0, d % 4))
        start(col(1, 0, 0), at(dx=d), ("p2", 1, d % 4))
    spread(0)
    start(head(0, 0, 0), at(dz=1), ("hz", 1, 0))
    start(head(0, 0, 1), at(dz=-1), ("hz", 7, 0))
    head_first()
    for d in (1, -1):
        arrive(col(0, 0, -d), sib, ("p2", 0, d % 4))
        start(mid_half(0, -d, d), at(dy=d), ("p2r", 0, d % 4))
        arrive(col(1, -d, 0), sib, ("p2", 1, d % 4))
        start(mid_half(1, -d, d), at(dx=d), ("p2r", 1, d % 4))
        spread(-d)
    second_hop(0)
    head_own(False)
    arrive(act.at[pl.ds(136, 8)], sib, ("halo", 0))
    arrive(act.at[pl.ds(0, 8)], sib, ("halo", 1))

    @pl.when(s == 0)
    def _():
        act[0:8, :] = jnp.zeros((8, CH), F32)

    @pl.when(s == 15)
    def _():
        act[136:144, :] = jnp.zeros((8, CH), F32)

    for d in (1, -1):
        arrive(mid_half(0, 2, d), sib, ("p2r", 0, d % 4))
        arrive(mid_half(1, 2, d), sib, ("p2r", 1, d % 4))
    spread(2)
    head_on()

    @rows_loop(BINS, 16)
    def _(r):
        for q in range(4):
            taps = [act[pl.ds(r + 8 * k, 16), pl.ds(q * 384, 384)] for k in range(3)]
            for i in range(4):
                g = 4 * q + i
                pieces = [t[:, 96 * i : 96 * i + 96] for t in taps] + [jnp.zeros((16, 96), F32)]
                AP[g % 2, g // 2, pl.ds(r, 16), :] = jnp.concatenate(pieces, axis=1).astype(BF16)

    start(AP.at[1 - c], sib, ("ax",), dst=AX)
    last_hop(0)
    head_second()
    second_hop(-1)
    second_hop(1)
    second_hop(2)
    head_third()
    last_hop(-1)
    last_hop(1)
    last_hop(2)
    from_sib()

    def w(p, j, cc):
        t = 3 * (j // 4) + p if p < 2 else 5 - 3 * (j // 4)
        return W[t, j % 4, cc].reshape(INNER, 128)

    conv[...] = jnp.zeros_like(conv)

    def conv_step(j, carry):
        two = [(2 * j + i, cc) for i in range(2) for cc in range(2)]
        lhs = jnp.concatenate([AP[cc, i] for i, cc in two], axis=1)
        rhs = jnp.concatenate([w(p, i, cc) for i, cc in two for p in range(3)], axis=1)
        conv[...] += lax.dot_general(lhs, rhs, LAST, preferred_element_type=F32)
        return carry

    lax.fori_loop(0, 4, conv_step, 0)
    for dy in (0, -1, 1):
        head_other(dy)

    @rows_loop(BINS, 16)
    def _(r):
        hidden[pl.ds(r, 16), :] = gelu(conv[pl.ds(r, 16), :]).astype(BF16)

    start(hidden, sib, ("hidden",), dst=dh2.at[0])

    for q in range(4):
        mixed = []
        for i in range(2):
            j = 2 * q + i
            rhs = jnp.concatenate([w(2, j, 0), w(2, j, 1)], axis=1)
            m = jnp.dot(hidden[...], rhs, preferred_element_type=F32)
            mixed += [m[:, 32:128], m[:, 160:256]]
        lanes = slice(384 * q, 384 * q + 384)
        tower[:, lanes] = (in_ref[:, lanes].astype(F32) + jnp.concatenate(mixed, axis=1)).astype(BF16)

    dtower[...] = jnp.zeros_like(dtower)
    cot_copy.wait()

    def head_step(zz, yy):
        lanes = pl.ds(pl.multiple_of((zz * 4 + yy) * 512, 512), 512)
        weight = jnp.concatenate([H[zz, yy, 0], H[zz, yy, 1]], axis=1)
        logits = jnp.dot(tower[...], weight, preferred_element_type=F32) + bias_ref[lanes].reshape(1, -1)
        e = jnp.exp(-jnp.abs(logits))
        pred_ref[:, lanes] = (jnp.maximum(logits, 0.0) + jnp.log1p(e)).astype(BF16)
        sigmoid = jnp.where(logits >= 0.0, 1.0, e) / (1.0 + e)
        dlogits = (cot_ref[:, lanes].astype(F32) * sigmoid).astype(BF16)
        dtower[...] += lax.dot_general(dlogits, weight, LAST, preferred_element_type=F32)

    def ready(dzl, dy):
        arrive(H.at[(zl + dzl) % 2, (y + dy) % 4, 1 - c], sib, ("hs", dzl, dy % 4))

    for dzl in (0, 1):
        for dy in (0, -1, 1, 2):
            ready(dzl, dy)
            head_step((zl + dzl) % 2, (y + dy) % 4)
            if dzl == 0 and dy == -1:
                head_other(2)
    out = pltpu.make_async_copy(pred_ref, pred_out, local.at[1])
    out.start()

    @rows_loop(BINS, 16)
    def _(r):
        for q in range(4):
            v = dtower[pl.ds(r, 16), pl.ds(q * 384, 384)]
            for i in range(4):
                g = 4 * q + i
                pieces = [jnp.zeros((16, 32), F32), v[:, 96 * i : 96 * i + 96]]
                DT[g % 2, g // 2, pl.ds(r, 16), :] = jnp.concatenate(pieces, axis=1).astype(BF16)

    start(DT.at[1 - c], sib, ("dt",), dst=DX)
    sum0[...] = jnp.zeros_like(sum0)

    def dhidden_step(j, carry):
        four = [(4 * j + i, cc) for i in range(4) for cc in range(2)]
        lhs = jnp.concatenate([DT[cc, i] for i, cc in four], axis=1)
        rhs = jnp.concatenate([w(2, i, cc) for i, cc in four], axis=1)
        sum0[...] += lax.dot_general(lhs, rhs, LAST, preferred_element_type=F32)
        return carry

    lax.fori_loop(0, 2, dhidden_step, 0)

    @rows_loop(BINS, 16)
    def _(r):
        d = sum0[pl.ds(r, 16), :] * gelu_slope(conv[pl.ds(r, 16), :])
        half = d.astype(BF16)
        dh2[2, pl.ds(r, 16), :] = half
        dext[pl.ds(r + 8, 16), :] = half.astype(F32)

    start(dh2.at[2], sib, ("dconv",), dst=dh2.at[1])
    start(dext.at[pl.ds(8, 8)], before, ("dhalo", 0), dst=dext.at[pl.ds(136, 8)])
    start(dext.at[pl.ds(128, 8)], after, ("dhalo", 1), dst=dext.at[pl.ds(0, 8)])

    arrive(dh2.at[0], sib, ("hidden",))
    hT[:, 0:128] = hidden[...].T
    hT[:, 128:256] = dh2[0].T
    dT[:, 0:128] = dh2[2].T
    arrive(AX, sib, ("ax",))
    arrive(DX, sib, ("dt",))
    arrive(dh2.at[1], sib, ("dconv",))
    dT[:, 128:256] = dh2[1].T

    def grad_step(i, carry):
        two = (2 * i, 2 * i + 1)
        rhs = [jnp.concatenate([AP[c, j], AX[j]], axis=0) for j in two]
        g = jnp.dot(dT[...], jnp.concatenate(rhs, axis=1), preferred_element_type=F32)
        rhs = [jnp.concatenate([DT[c, j], DX[j]], axis=0) for j in two]
        more = jnp.dot(hT[...], jnp.concatenate(rhs, axis=1), preferred_element_type=F32)
        for n, j in enumerate(two):
            for p in range(3):
                part = g[:, 384 * n + 128 * p : 384 * n + 128 * p + 128]
                if p == 2:
                    part = part + more[:, 128 * n : 128 * n + 128]
                G[p, j // 4, j % 4] = part.astype(BF16).reshape(4, 4, 48, 128)
        return carry

    lax.fori_loop(0, 4, grad_step, 0)

    def dact_prepare():
        arrive(dext.at[pl.ds(136, 8)], sib, ("dhalo", 0))
        arrive(dext.at[pl.ds(0, 8)], sib, ("dhalo", 1))

        @pl.when(s == 0)
        def _():
            dext[0:8, :] = jnp.zeros((8, INNER), F32)

        @pl.when(s == 15)
        def _():
            dext[136:144, :] = jnp.zeros((8, INNER), F32)

        dext16[...] = dext[...].astype(BF16)

    def dact_part(q):
        pieces = []
        for i in range(2):
            j = 2 * q + i
            for cc in range(2):
                rhs = jnp.concatenate([w(p, j, cc) for p in range(3)], axis=1)
                d = jnp.dot(dext16[...], rhs, preferred_element_type=F32)
                pieces.append(d[16:144, 0:96] + d[8:136, 96:192] + d[0:128, 192:288])
        dact[:, 384 * q : 384 * q + 384] = jnp.concatenate(pieces, axis=1)

    def dact_finish():
        @rows_loop(BINS, 16)
        def _(r):
            v = in_ref[pl.ds(r, 16), :].astype(F32)
            rs = lax.rsqrt(jnp.mean(v * v, axis=-1, keepdims=True) + 1e-06)
            gain = gain_ref[...].reshape(1, CH)
            dz = dact[pl.ds(r, 16), :] * gelu_slope(v * rs * gain) * gain
            dot = jnp.mean(dz * v, axis=-1, keepdims=True)
            ig = dtower[pl.ds(r, 16), :] + dz * rs - v * (rs * rs * rs * dot)
            ig_ref[pl.ds(r, 16), :] = ig.astype(BF16)

    jobs = [dact_prepare] + [functools.partial(dact_part, q) for q in range(4)] + [dact_finish]

    def half_x(m, h):
        return G.at[0, h, :, :, (x + m) % 4]

    def half_y(m, h):
        return G.at[1, h, (y + m) % 4]

    def half_z(m, h):
        zz = (z + m) % 8
        return G.at[2, zz % 2, pl.ds(2 * h, 2), zz // 2]

    def slots(ring):
        return [(0, m) for m in range(ring, 0, -1)], [(1, m) for m in range(ring - 1, 0, -1)]

    def order(n):
        seq = []
        for m in range(n // 2, 0, -1):
            seq.append((0, m))
            if m > 1:
                seq.append((1, m - 1))
        return seq

    rings = {"x": (4, half_x, RX, "dx"), "y": (4, half_y, RY, "dy"), "z": (8, half_z, RZ, "dz")}

    def ring_send(ax, d, k):
        n, block, buf, name = rings[ax]
        h, m = order(n)[k]
        h = h if d < 0 else 1 - h
        start(block(d * m, h), at(**{name: d}), ("r" + ax, d, k), dst=buf.at[(d + 1) // 2, k])

    def add(dst, srcs):
        total = dst[...].astype(F32)
        for src in srcs:
            total = total + src[...].astype(F32)
        dst[...] = total.astype(BF16)

    def ring_receive(ax, d, k):
        n, block, buf, name = rings[ax]
        seq = order(n)
        h, m = seq[k]
        slot = buf.at[(d + 1) // 2, k]
        arrive(slot, sib, ("r" + ax, d, k))
        mine = h if d < 0 else 1 - h
        add(block(d * (m - 1), mine), [slot])
        if m > 1:
            ring_send(ax, d, seq.index((h, m - 1)))

    for ax in "xyz":
        for d in (-1, 1):
            ring_send(ax, d, 0)
            ring_send(ax, d, 1)
    jobs.pop(0)()
    jobs.pop(0)()

    def both(ax, k):
        for d in (-1, 1):
            ring_receive(ax, d, k)

    both("z", 0)
    both("x", 0)
    both("y", 0)
    both("z", 1)
    jobs.pop(0)()
    both("z", 2)
    both("x", 1)
    both("y", 1)
    both("z", 3)
    jobs.pop(0)()
    both("z", 4)
    both("x", 2)
    both("y", 2)

    def mid_send(p, d):
        if p == 0:
            start(G.at[0, :, (y + d) % 4, :, x], at(dy=d), ("m", 0, d), dst=M0.at[d - 1])
        elif p == 1:
            start(G.at[1, :, y, :, (x + d) % 4], at(dx=d), ("m", 1, d), dst=M1.at[d - 1])
        else:
            start(G.at[2, zl, :, zh, (x + d) % 4], at(dx=d), ("m", 2, d), dst=M2.at[d - 1])

    def mid_receive(p):
        buf = (M0, M1, M2)[p]
        for d in (1, 2, 3):
            arrive(buf.at[d - 1], sib, ("m", p, d))
        home = (G.at[0, :, y, :, x], G.at[1, :, y, :, x], G.at[2, zl, :, zh, x])[p]
        add(home, [buf.at[d] for d in range(3)])

    for p in (0, 1):
        for d in (1, 2, 3):
            mid_send(p, d)
    both("z", 5)
    both("z", 6)
    for d in (1, 2, 3):
        mid_send(2, d)
    jobs.pop(0)()

    def last_send(p, d):
        if p < 2:
            zz = (z + d) % 8
            start(G.at[p, zz % 2, y, zz // 2, x], at(dz=d), ("l", p, d), dst=(L0, L1)[p].at[d - 1])
        else:
            start(G.at[2, zl, (y + d) % 4, zh, x], at(dy=d), ("l", 2, d), dst=L2.at[d - 1])

    def last_receive(p):
        buf, n = ((L0, 7), (L1, 7), (L2, 3))[p]
        for d in range(n):
            arrive(buf.at[d], sib, ("l", p, d + 1))
        total = G[p, zl, y, zh, x].astype(F32)
        for d in range(n):
            total = total + buf[d].astype(F32)
        grad_ref[p] = total * (1.0 / 16.0)

    for p in (0, 1):
        mid_receive(p)
        for d in range(1, 8):
            last_send(p, d)
    mid_receive(2)
    for d in (1, 2, 3):
        last_send(2, d)
    while jobs:
        jobs.pop(0)()
    for p in range(3):
        last_receive(p)
    copies.of(W.at[:, :, c], W.at[:, :, c], sib, ("s",)).wait_send()
    copies.finish()
    out.wait()
    assert len(copies.ids) == N_COPIES, len(copies.ids)


def finish_kernel(pred_ref, ig_ref, grad_ref, pred_out, ig_out, conv_out, mix_out):
    pred_out[...] = pred_ref[...]
    ig_out[...] = ig_ref[...]

    @pl.when(pl.program_id(0) == 0)
    def _():
        packed = jnp.concatenate([grad_ref[p] for p in range(3)], axis=1)
        for k in range(3):
            conv_out[k] = packed[:, 96 * k : 96 * k + 96]
        mix_out[...] = packed[:, 288:384]


def body(tower_input, norm_gain, conv_weight, mix_weight, head_weight, head_bias, pred_cotangent):
    vmem = pl.BlockSpec(memory_space=pltpu.VMEM)
    hbm = pl.BlockSpec(memory_space=pl.ANY)
    scratch = [
        ((6, 4, 2, 4, 4, 48, 128), BF16),
        ((2, 4, 2, CH, 256), BF16),
        ((BINS + 16, CH), F32),
        ((2, 8, BINS, 384), BF16),
        ((8, BINS, 384), BF16),
        ((BINS, INNER), F32),
        ((BINS, INNER), BF16),
        ((BINS, CH), BF16),
        ((BINS, CH), F32),
        ((2, 8, BINS, 128), BF16),
        ((8, BINS, 128), BF16),
        ((BINS + 16, INNER), F32),
        ((BINS + 16, INNER), BF16),
        ((INNER, 256), BF16),
        ((INNER, 256), BF16),
        ((3, BINS, INNER), BF16),
        ((BINS, CH), F32),
        ((BINS, TRACKS), BF16),
        ((BINS, TRACKS), BF16),
        ((3, 2, 4, 4, 4, 48, 128), BF16),
        ((2, 3, 4, 4, 48, 128), BF16),
        ((2, 3, 4, 4, 48, 128), BF16),
        ((2, 7, 2, 4, 48, 128), BF16),
        ((3, 2, 4, 48, 128), BF16),
        ((3, 2, 4, 48, 128), BF16),
        ((3, 4, 48, 128), BF16),
        ((7, 48, 128), BF16),
        ((7, 48, 128), BF16),
        ((3, 48, 128), BF16),
        ((BINS, INNER), F32),
    ]
    predictions, input_grad, grads = pl.pallas_call(
        kernel,
        out_shape=[
            jax.ShapeDtypeStruct((BINS, TRACKS), BF16),
            jax.ShapeDtypeStruct((BINS, CH), BF16),
            jax.ShapeDtypeStruct((3, 48, 128), F32),
        ],
        in_specs=[vmem, vmem, hbm, vmem, vmem, vmem, hbm],
        out_specs=[hbm, vmem, vmem],
        scratch_shapes=[pltpu.VMEM(*spec) for spec in scratch]
        + [
            pltpu.SemaphoreType.DMA((N_COPIES,)),
            pltpu.SemaphoreType.DMA((N_COPIES,)),
            pltpu.SemaphoreType.DMA((3,)),
        ],
        compiler_params=pltpu.CompilerParams(
            collective_id=0, has_side_effects=True, vmem_limit_bytes=60 * 2**20
        ),
        name="block",
    )(
        conv_weight.transpose(0, 2, 1),
        mix_weight,
        head_weight,
        tower_input[0],
        norm_gain,
        head_bias,
        pred_cotangent[0],
    )
    predictions, input_grad, conv_grad, mix_grad = pl.pallas_call(
        finish_kernel,
        out_shape=[
            jax.ShapeDtypeStruct((BINS, TRACKS), BF16),
            jax.ShapeDtypeStruct((BINS, CH), BF16),
            jax.ShapeDtypeStruct((3, 48, 96), F32),
            jax.ShapeDtypeStruct((48, 96), F32),
        ],
        grid=(4,),
        in_specs=[
            pl.BlockSpec((32, TRACKS), lambda i: (i, 0)),
            pl.BlockSpec((32, CH), lambda i: (i, 0)),
            pl.BlockSpec((3, 48, 128), lambda i: (0, 0, 0)),
        ],
        out_specs=[
            pl.BlockSpec((32, TRACKS), lambda i: (i, 0)),
            pl.BlockSpec((32, CH), lambda i: (i, 0)),
            pl.BlockSpec((3, 48, 96), lambda i: (0, 0, 0)),
            pl.BlockSpec((48, 96), lambda i: (0, 0)),
        ],
        name="unpack",
    )(predictions, input_grad, grads)
    return (predictions[None], input_grad[None], conv_grad.transpose(0, 2, 1), mix_grad)


def solution(mesh):
    in_specs = (
        P("batch", "seq", None),
        P(),
        P(None, "seq", "batch"),
        P("batch", "seq"),
        P(None, "seq"),
        P(),
        P("batch", "seq", None),
    )
    out_specs = (
        P("batch", "seq", None),
        P("batch", "seq", None),
        P(None, "seq", "batch"),
        P("batch", "seq"),
    )
    return jax.shard_map(body, mesh=mesh, in_specs=in_specs, out_specs=out_specs, check_vma=False)
```
